32 devices in a mesh: parts: 2 (over x), seq: 16 (over z, y, core).
Axes of the slice: x: 2, y: 2, z: 4, core: 2. Of those that a mesh axis runs over, the one named last changes fastest.
Arguments:
- proj_main: bfloat16 [2, 4096, 4096], P(None, ('parts', 'seq')), parts along dimension 1, may hold values from -6 to 6
- proj_state: bfloat16 [2, 4096, 128], P(None, ('parts', 'seq')), parts along dimension 1, may hold values from -6 to 6
- step_raw: float32 [2, 4096, 16], P(None, ('parts', 'seq')), parts along dimension 1, may hold values from -0.5 to 1.5
- step_bias: float32 [16], replicated, may hold values from -6.5 to -5.5
- decay_log: float32 [16], replicated, may hold values from -10 to 3
- skip_scale: float32 [16], replicated, may hold values from 0.5 to 2
- norm_gain: float32 [2048], replicated, may hold values from 0.1 to 1.9
- out_weight: bfloat16 [2048, 1024], P('seq'), may hold values from -0.125 to 0.125
- grad_mixed: bfloat16 [4096, 1024], P(('parts', 'seq')), parts along dimension 0, may hold values from -6 to 6
Outputs:
- mixed_out: bfloat16 [4096, 1024], P(('parts', 'seq')), parts along dimension 0
- grad_main: bfloat16 [2, 4096, 4096], P(None, ('parts', 'seq')), parts along dimension 1
- grad_state: float32 [2, 4096, 128], P(None, ('parts', 'seq')), parts along dimension 1
- grad_step: float32 [2, 4096, 16], P(None, ('parts', 'seq')), parts along dimension 1
- grad_weight: float32 [4096, 1024], P(('parts', 'seq')), parts along dimension 0
The draws below stay inside these ranges and needn't reach their ends.
There are 2 independent parts, one for each index of `parts`. The reference program is written for one: setup_inputs(seed, part) draws one part's arguments, and reference() takes and returns one part's arrays. A program takes and returns all parts, laid end to end along the dimension named above; an argument that names none is the same for every part. Nothing has to cross between parts.
All inputs are finite; a program needn't handle non-finite values.
Results may differ from the reference program's by a relative error of at most 0.0059.
Values may be sent and summed in bfloat16 or wider, within the bound.
A program may use at most 128 MiB of HBM per device.

```python
import math
import jax
import jax.numpy as jnp
from jax import lax

D = 1024
HEADS = 16
HEAD_DIM = 128
STATE = 64
BLOCK = 128
TOK_DEV = 128
INNER = 2048
LENGTH = 2048


def draw_step_raw(key, part):
    first_key, second_key = jax.random.split(key)
    device_blocks = LENGTH // TOK_DEV
    offset = jax.random.uniform(first_key, (2, device_blocks, 1, HEADS), jnp.float32, 0.0, 1.0)
    noise = jax.random.uniform(second_key, (2, device_blocks, TOK_DEV, HEADS), jnp.float32, -0.5, 0.5)
    return (offset + noise).reshape(2, LENGTH, HEADS)


def draw_decay_log(key, part):
    first_key, second_key, third_key = jax.random.split(key, 3)
    order = jax.random.permutation(first_key, HEADS)
    quick_count = HEADS // 2
    quick = order < quick_count
    slow_rate = jnp.exp(jax.random.uniform(second_key, (HEADS,), jnp.float32, math.log(0.1), math.log(1.5))) / LENGTH
    quick_rate = jnp.exp(jax.random.uniform(third_key, (HEADS,), jnp.float32, math.log(1.0 / 50.0), math.log(1.0 / 30.0)))
    per_step = jnp.where(quick, quick_rate, slow_rate)
    return jnp.log(per_step / 0.004)


def levels(rng, shape, pieces, smallest, largest):
    factor_of = 1.0
    for position, parts in pieces:
        draws = jax.random.uniform(jax.random.fold_in(jax.random.fold_in(rng, 6), position), (parts,), jnp.float32, smallest / len(pieces), largest / len(pieces))
        factor_of = factor_of * jnp.repeat(jnp.exp(draws), shape[position] // parts).reshape((-1,) + (1,) * (len(shape) - 1 - position))
    return factor_of


def scatter_about(rng, shape, scale, most, pieces=(), held_as=jnp.bfloat16):
    values = jax.random.normal(rng, shape, jnp.float32) * scale
    if len(pieces) > 0:
        values = levels(rng, shape, pieces, -0.22, 0.18) * values
    return jnp.clip(values, min=-most, max=most).astype(held_as)


def setup_inputs(seed: int = 0, part: int = 0) -> dict:
    arg_keys = jax.random.split(jax.random.key(seed), 10)
    part_keys = jax.random.split(jax.random.fold_in(arg_keys[9], part), 10)
    proj_main = scatter_about(part_keys[0], (2, LENGTH, 2 * INNER), 1.0, 6.0, ((1, 16),))
    proj_state = scatter_about(part_keys[1], (2, LENGTH, 2 * STATE), 1.0, 6.0, ((1, 16),))
    step_raw = draw_step_raw(jax.random.fold_in(jax.random.fold_in(arg_keys[9], part), 71), part)
    step_bias = jnp.clip(jax.random.uniform(arg_keys[3], (HEADS,), jnp.float32, -6.5, -5.5), -6.5, -5.5)
    decay_log = draw_decay_log(jax.random.fold_in(arg_keys[9], 71), part)
    skip_scale = jnp.clip(jnp.exp(jax.random.uniform(arg_keys[5], (HEADS,), jnp.float32, math.log(0.5), math.log(2.0))), 0.5, 2.0)
    norm_gain = jnp.clip(1.0 + 0.18 * jax.random.normal(arg_keys[6], (INNER,), jnp.float32), 0.1, 1.9)
    out_weight = scatter_about(arg_keys[7], (INNER, D), INNER ** -0.5, 0.125, ((0, 16),))
    grad_mixed = scatter_about(part_keys[8], (LENGTH, D), 1.0, 6.0, ((0, 16),))
    return dict(proj_main=proj_main, proj_state=proj_state, step_raw=step_raw, step_bias=step_bias, decay_log=decay_log, skip_scale=skip_scale, norm_gain=norm_gain, out_weight=out_weight, grad_mixed=grad_mixed)


PRECISE = lax.Precision.HIGHEST
EPSILON = 1e-05

def block_step(carry_state, block_data):
    x_part, b_part, c_part, rate_part, step_part = block_data
    cumulative = jnp.cumsum(rate_part, axis=0)
    positions = jnp.arange(rate_part.shape[0])
    lower_mask = (positions[:, None] >= positions[None, :])[:, :, None]
    gaps_log = cumulative[:, None, :] - cumulative[None, :, :]
    decay_mat = jnp.where(lower_mask, jnp.exp(jnp.where(lower_mask, gaps_log, 0.0)), 0.0)
    scores = jnp.dot(c_part, b_part.T, precision=PRECISE)
    mixing = scores[:, :, None] * decay_mat * step_part[None, :, :]
    inside = jnp.einsum('tuh,uhp->thp', mixing, x_part, precision=PRECISE)
    carried = jnp.exp(cumulative)[:, :, None] * jnp.einsum('tn,hpn->thp', c_part, carry_state, precision=PRECISE)
    weighting = jnp.exp(cumulative[-1][None, :] - cumulative) * step_part
    fresh = jnp.einsum('uhp,un->hpn', weighting[:, :, None] * x_part, b_part, precision=PRECISE)
    next_state = jnp.exp(cumulative[-1])[:, None, None] * carry_state + fresh
    return (next_state, inside + carried)

def strand_scan(x_vals, b_vals, c_vals, rate_vals, step_vals, block_len):
    blocks_count = x_vals.shape[0] // block_len
    pieces_all = tuple((array_in.reshape((blocks_count, block_len) + array_in.shape[1:]) for array_in in (x_vals, b_vals, c_vals, rate_vals, step_vals)))
    zero_state = jnp.zeros((x_vals.shape[1], x_vals.shape[2], b_vals.shape[1]), x_vals.dtype)
    last_state, outputs = lax.scan(block_step, zero_state, pieces_all)
    return (outputs.reshape(x_vals.shape), last_state)

def strand_core(x_vals, b_vals, c_vals, step_raw, step_bias, decay_log, skip_scale):
    step_vals = jax.nn.softplus(step_raw + step_bias)
    rate_vals = -jnp.exp(decay_log) * step_vals
    y_local, last_state = strand_scan(x_vals, b_vals, c_vals, rate_vals, step_vals, BLOCK)
    cumulative = jnp.cumsum(rate_vals, axis=0)
    return (y_local + skip_scale[:, None] * x_vals, last_state, cumulative[-1], cumulative)

def gate_norm(y_vals, z_vals, norm_gain):
    flat_y = y_vals.reshape(y_vals.shape[0], -1)
    gated = flat_y * jax.nn.silu(z_vals)
    return gated * lax.rsqrt(lax.optimization_barrier(jnp.mean(gated * gated, axis=-1, keepdims=True)) + EPSILON) * norm_gain

def reference(proj_main, proj_state, step_raw, step_bias, decay_log, skip_scale, norm_gain, out_weight, grad_mixed):
    x_vals = proj_main[:, :, :INNER].astype(jnp.float32).reshape(2, LENGTH, HEADS, HEAD_DIM)
    z_vals = proj_main[:, :, INNER:].astype(jnp.float32)
    b_vals = proj_state[:, :, :STATE].astype(jnp.float32)
    c_vals = proj_state[:, :, STATE:].astype(jnp.float32)

    def core_fn(x_in, b_in, c_in, raw_in):
        return jax.vmap(lambda x_one, b_one, c_one, raw_one: strand_core(x_one, b_one, c_one, raw_one, step_bias, decay_log, skip_scale)[0])(x_in, b_in, c_in, raw_in)
    y_vals, core_back = jax.vjp(core_fn, x_vals, b_vals, c_vals, step_raw)

    def norm_fn(y_in, z_in):
        return jax.vmap(gate_norm, in_axes=(0, 0, None))(y_in, z_in, norm_gain)
    normed, norm_back = jax.vjp(norm_fn, y_vals, z_vals)
    normed_low = normed.astype(jnp.bfloat16)
    strand_out = jnp.stack([jnp.dot(normed_low[strand], out_weight, preferred_element_type=jnp.float32) for strand in range(2)]).astype(jnp.bfloat16)
    mixed_out = (strand_out[0].astype(jnp.float32) + strand_out[1, ::-1, ::-1].astype(jnp.float32)).astype(jnp.bfloat16)
    backward_in = jnp.stack([grad_mixed, grad_mixed[::-1, ::-1]])
    grad_weight = jnp.dot(normed_low.reshape(2 * LENGTH, INNER).T, backward_in.reshape(2 * LENGTH, D), preferred_element_type=jnp.float32)
    grad_normed = jnp.stack([jnp.dot(backward_in[strand], out_weight.T, preferred_element_type=jnp.float32) for strand in range(2)])
    grad_y, grad_z = norm_back(grad_normed)
    grad_x, grad_b, grad_c, grad_step = core_back(grad_y)
    grad_main = jnp.concatenate([grad_x.reshape(2, LENGTH, INNER), grad_z], axis=-1).astype(jnp.bfloat16)
    grad_state = jnp.concatenate([grad_b, grad_c], axis=-1)
    return (mixed_out, grad_main, grad_state, grad_step, grad_weight)
```

```python
import functools

import jax
import jax.numpy as jnp
from jax import lax
from jax.experimental import pallas as pl
from jax.experimental.pallas import tpu as pltpu
from jax.sharding import PartitionSpec as P

D = 1024
HEADS = 16
HEAD_DIM = 128
STATE = 64
INNER = 2048
TOK = 128
LANES = 128
ROWS = 2 * HEADS * STATE
EPSILON = 1e-05
HIGH = lax.Precision.HIGHEST
F32 = jnp.float32
BF16 = jnp.bfloat16
MESH = pl.DeviceIdType.MESH
VMEM_LIMIT = 56 * 2**20


def dot(a, b, ca=1, cb=0, precision=None):
    return lax.dot_general(
        a, b, (((ca,), (cb,)), ((), ())), precision=precision, preferred_element_type=F32
    )


def grids(shape=(TOK, TOK)):
    return lax.broadcasted_iota(jnp.int32, shape, 0), lax.broadcasted_iota(jnp.int32, shape, 1)


def anti_identity():
    row, col = grids()
    return (row + col == TOK - 1).astype(BF16)


def flip_both(block):
    anti = anti_identity()
    turned = dot(anti, block).astype(BF16)
    count = block.shape[1] // TOK
    parts = [
        dot(turned[:, (count - 1 - k) * TOK : (count - k) * TOK], anti).astype(BF16)
        for k in range(count)
    ]
    return jnp.concatenate(parts, axis=1)


def steps(raw, bias, dlog):
    arg = raw + bias
    size = jnp.maximum(arg, 0.0) + jnp.log1p(jnp.exp(-jnp.abs(arg)))
    rate = -jnp.exp(dlog) * size
    row, col = grids()
    lower = (row >= col).astype(F32)
    cum = dot(lower, rate, precision=HIGH)
    return arg, size, rate, cum


def head(h):
    return slice(h * HEAD_DIM, (h + 1) * HEAD_DIM)


def srows(h):
    return slice(h * STATE, (h + 1) * STATE)


def local_state_kernel(x_ref, bc_ref, raw_ref, bias_ref, dlog_ref, st_ref, dec_ref):
    _, size, _, cum = steps(raw_ref[0], bias_ref[...], dlog_ref[...])
    total = cum[TOK - 1 : TOK, :]
    weight = jnp.exp(total - cum) * size
    b = bc_ref[0, :, :STATE]
    for h in range(HEADS):
        xw = (x_ref[0, :, head(h)].astype(F32) * weight[:, h : h + 1]).astype(BF16)
        st_ref[0, srows(h), :] = dot(b, xw, 0, 0).astype(BF16)
    dec_ref[0] = jnp.exp(total)


def mixing(scores, mask, cum, cum_t, size_t, h):
    gap = cum[:, h : h + 1] - cum_t[h : h + 1, :]
    decay = jnp.where(mask, jnp.exp(jnp.minimum(gap, 0.0)), 0.0)
    return decay * size_t[h : h + 1, :]


def middle_kernel(
    main_ref, bc_ref, raw_ref, bias_ref, dlog_ref, skip_ref, gain_ref, w_ref, gm_ref, gmm_ref, e_ref,
    nt_ref, so_ref, gz_ref, gy_ref, de_ref, gyy_ref,
    y_s, gn_s, bi_s, no_s,
):
    strand = pl.program_id(0)

    @pl.when(strand == 0)
    def _():
        bi_s[...] = gm_ref[...]

    @pl.when(strand == 1)
    def _():
        bi_s[...] = flip_both(gmm_ref[...])

    gn_s[...] = dot(bi_s[...], w_ref[...], 1, 1) * gain_ref[...]
    _, size, _, cum = steps(raw_ref[0], bias_ref[...], dlog_ref[...])
    cum_t, size_t = cum.T, size.T
    ecum = jnp.exp(cum)
    b, c = bc_ref[0, :, :STATE], bc_ref[0, :, STATE:]
    scores = dot(c, b, 1, 1)
    row, col = grids()
    mask = row >= col
    squares = jnp.zeros((TOK, LANES), F32)
    crossed = jnp.zeros((TOK, LANES), F32)
    for h in range(HEADS):
        m = (scores * mixing(scores, mask, cum, cum_t, size_t, h)).astype(BF16)
        x = main_ref[0, :, head(h)]
        y = dot(m, x) + ecum[:, h : h + 1] * dot(c, e_ref[0, srows(h), :])
        y = y + skip_ref[0:1, h : h + 1] * x.astype(F32)
        y_s[:, head(h)] = y
        z = main_ref[0, :, INNER + h * HEAD_DIM : INNER + (h + 1) * HEAD_DIM].astype(F32)
        gated = y * (z / (1.0 + jnp.exp(-z)))
        squares += gated * gated
        crossed += gated * gn_s[:, head(h)]
    r = lax.rsqrt(jnp.sum(squares, axis=1, keepdims=True) / INNER + EPSILON)
    factor = r * r * r * (jnp.sum(crossed, axis=1, keepdims=True) / INNER)
    spin = jnp.where(strand == 0, (row == col).astype(F32), (row + col == TOK - 1).astype(F32))
    spin = spin.astype(BF16)
    for h in range(HEADS):
        z = main_ref[0, :, INNER + h * HEAD_DIM : INNER + (h + 1) * HEAD_DIM].astype(F32)
        y = y_s[:, head(h)]
        sig = 1.0 / (1.0 + jnp.exp(-z))
        silu = z * sig
        gated = y * silu
        normed = (gated * r * gain_ref[:, head(h)]).astype(BF16)
        no_s[:, head(h)] = normed
        nt_ref[head(h), :] = dot(normed, spin, 0, 0).astype(BF16)
        dgated = r * gn_s[:, head(h)] - gated * factor
        gz_ref[0, :, head(h)] = (dgated * y * (sig * (1.0 + z * (1.0 - sig)))).astype(BF16)
        gy = (dgated * silu).astype(BF16)
        gy_ref[0, :, head(h)] = gy
        gyf = gy.astype(F32)
        scan_y = y - skip_ref[0:1, h : h + 1] * main_ref[0, :, head(h)].astype(F32)
        gyy_ref[0, :, h : h + 1] = jnp.sum(gyf * scan_y, axis=1, keepdims=True)
        de_ref[0, srows(h), :] = dot(c, (gyf * ecum[:, h : h + 1]).astype(BF16), 0, 0).astype(BF16)
    so_ref[0] = dot(no_s[...], w_ref[...]).astype(BF16)


def last_kernel(
    x_ref, gz_ref, gy_ref, bc_ref, raw_ref, bias_ref, dlog_ref, skip_ref, e_ref, lv_ref, gyy_ref,
    gmain_ref, gstate_ref, gstep_ref,
    xdx_s,
):
    arg, size, _, cum = steps(raw_ref[0], bias_ref[...], dlog_ref[...])
    cum_t, size_t = cum.T, size.T
    ecum = jnp.exp(cum)
    total = cum[TOK - 1 : TOK, :]
    weight = jnp.exp(total - cum) * size
    b, c = bc_ref[0, :, :STATE], bc_ref[0, :, STATE:]
    scores = dot(c, b, 1, 1)
    row, col = grids()
    mask = row >= col
    lane = lax.broadcasted_iota(jnp.int32, (1, LANES), 1)
    gscore = jnp.zeros((TOK, TOK), F32)
    gb = jnp.zeros((TOK, STATE), F32)
    gc = jnp.zeros((TOK, STATE), F32)
    gtotal = jnp.zeros((1, LANES), F32)
    xdx_s[...] = jnp.zeros_like(xdx_s)
    for h in range(HEADS):
        w = mixing(scores, mask, cum, cum_t, size_t, h)
        m = (scores * w).astype(BF16)
        x, gy = x_ref[0, :, head(h)], gy_ref[0, :, head(h)]
        xf, gyf = x.astype(F32), gy.astype(F32)
        lv, e = lv_ref[0, srows(h), :], e_ref[0, srows(h), :]
        gscore += dot(gy, x, 1, 1) * w
        wcol = weight[:, h : h + 1]
        through = wcol * dot(b, lv)
        dx = dot(m, gy, 0, 0) + through
        gmain_ref[0, :, head(h)] = (dx + skip_ref[0:1, h : h + 1] * gyf).astype(BF16)
        xdx_s[:, h : h + 1] = jnp.sum(xf * dx, axis=1, keepdims=True)
        gc += dot((gyf * ecum[:, h : h + 1]).astype(BF16), e, 1, 1)
        gb += dot((xf * wcol).astype(BF16), lv, 1, 1)
        held = jnp.sum(xf * through, axis=0, keepdims=True)
        kept = jnp.sum(e.astype(F32) * lv.astype(F32), axis=0, keepdims=True)
        both = jnp.sum(held + jnp.exp(total[:, h : h + 1]) * kept, axis=1, keepdims=True)
        gtotal += jnp.where(lane == h, both, 0.0)
    gs = gscore.astype(BF16)
    gstate_ref[0, :, :STATE] = gb + dot(gs, c, 0, 0)
    gstate_ref[0, :, STATE:] = gc + dot(gs, b)
    gmain_ref[0, :, INNER:] = gz_ref[0]
    real = lane < HEADS
    gcum = jnp.where(real, gyy_ref[0], 0.0) - xdx_s[...]
    upper = (row <= col).astype(F32)
    grate = dot(upper, gcum, precision=HIGH) + gtotal
    gsize = xdx_s[...] / size - jnp.exp(dlog_ref[...]) * grate
    gstep_ref[0] = gsize / (1.0 + jnp.exp(-arg))


def weight_kernel(n, nt_ref, gm_ref, so_ref, som_ref, gw_ref, mixed_ref):
    plain = jnp.zeros(gw_ref.shape, F32)
    turned = jnp.zeros(gw_ref.shape, F32)

    def body(i, held):
        plain, turned = held
        near = gm_ref[pl.ds(pl.multiple_of(i * TOK, TOK), TOK), :]
        far = gm_ref[pl.ds(pl.multiple_of((n - 1 - i) * TOK, TOK), TOK), :]
        return plain + dot(nt_ref[i, :, :TOK], near), turned + dot(nt_ref[i, :, TOK:], far)

    plain, turned = lax.fori_loop(0, n, body, (plain, turned))
    row, col = grids()
    anti = (row + col == TOK - 1).astype(F32)
    count = D // TOK
    for k in range(count):
        back = turned[:, (count - 1 - k) * TOK : (count - k) * TOK]
        gw_ref[:, k * TOK : (k + 1) * TOK] = plain[:, k * TOK : (k + 1) * TOK] + dot(
            back, anti, precision=HIGH
        )
    mixed_ref[...] = (so_ref[...].astype(F32) + flip_both(som_ref[...]).astype(F32)).astype(BF16)


def exchange_kernel(n, backward, *refs):
    if backward:
        (st_ref, dec_ref, block_ref, nt_ref, out_ref, gotblock_ref, gotnt_ref, inbox, outbox) = refs[:9]
        sems = refs[9:]
        st_send, st_recv, out_send, out_recv, block_send, block_recv, nt_send, nt_recv = sems
        decbox = dec_ref
    else:
        (st_ref, dec_ref, block_ref, out_ref, gotblock_ref, decbox, inbox, outbox) = refs[:8]
        sems = refs[8:]
        st_send, st_recv, out_send, out_recv, block_send, block_recv, dec_send, dec_recv = sems
    me = lax.axis_index("seq")
    share = ROWS // n
    inner = INNER // n
    barrier = pltpu.get_barrier_semaphore()

    def greet(k, _):
        pl.semaphore_signal(
            barrier, inc=1, device_id={"seq": lax.rem(me + k, n)}, device_id_type=MESH
        )
        return 0

    lax.fori_loop(1, n, greet, 0)
    pl.semaphore_wait(barrier, n - 1)

    def rows_of(i, size):
        return pl.ds(pl.multiple_of(i * size, size), size)

    def st_copy(to, slot):
        return pltpu.make_async_remote_copy(
            src_ref=st_ref.at[rows_of(to, share), :], dst_ref=inbox.at[slot],
            send_sem=st_send.at[to], recv_sem=st_recv.at[slot],
            device_id={"seq": to}, device_id_type=MESH,
        )

    def dec_copy(to, slot):
        return pltpu.make_async_remote_copy(
            src_ref=dec_ref.at[to], dst_ref=decbox.at[slot],
            send_sem=dec_send.at[to], recv_sem=dec_recv.at[slot],
            device_id={"seq": to}, device_id_type=MESH,
        )

    def nt_copy(to, slot):
        return pltpu.make_async_remote_copy(
            src_ref=nt_ref.at[rows_of(to, inner), :], dst_ref=gotnt_ref.at[slot],
            send_sem=nt_send.at[to], recv_sem=nt_recv.at[slot],
            device_id={"seq": to}, device_id_type=MESH,
        )

    def out_copy(to, slot):
        return pltpu.make_async_remote_copy(
            src_ref=outbox.at[to], dst_ref=out_ref.at[rows_of(slot, share), :],
            send_sem=out_send.at[to], recv_sem=out_recv.at[slot],
            device_id={"seq": to}, device_id_type=MESH,
        )

    def start_st(k, _):
        to = lax.rem(me + k, n)
        if not backward:
            dec_copy(to, me).start()
        st_copy(to, me).start()
        return 0

    lax.fori_loop(1, n, start_st, 0)
    block_copy = pltpu.make_async_remote_copy(
        src_ref=block_ref, dst_ref=gotblock_ref, send_sem=block_send, recv_sem=block_recv,
        device_id={"seq": n - 1 - me}, device_id_type=MESH,
    )
    block_copy.start()
    if backward:
        lax.fori_loop(1, n, lambda k, _: (nt_copy(lax.rem(me + k, n), me).start(), 0)[1], 0)
        gotnt_ref[me] = nt_ref[rows_of(me, inner), :]
    else:
        decbox[me] = dec_ref[me]
    inbox[me] = st_ref[rows_of(me, share), :]

    def arrive(k, _):
        other = lax.rem(me + k, n)
        if not backward:
            dec_copy(other, other).wait_recv()
        st_copy(other, other).wait_recv()
        return 0

    lax.fori_loop(1, n, arrive, 0)

    groups = max(1, share // STATE)
    size = share // groups

    def scan(k, held):
        i = n - 1 - k if backward else k
        outbox[i] = held.astype(BF16)

        @pl.when(i != me)
        def _():
            out_copy(i, me).start()

        grown = [
            held[g * size : (g + 1) * size] * decbox[i, g : g + 1, :] for g in range(groups)
        ]
        grown = grown[0] if groups == 1 else jnp.concatenate(grown, axis=0)
        return grown + inbox[i].astype(F32)

    lax.fori_loop(0, n, scan, jnp.zeros((share, LANES), F32))
    out_ref[rows_of(me, share), :] = outbox[me]

    def finish(k, _):
        other = lax.rem(me + k, n)
        out_copy(other, other).wait_recv()
        out_copy(other, me).wait_send()
        st_copy(other, me).wait_send()
        if backward:
            nt_copy(other, other).wait_recv()
            nt_copy(other, me).wait_send()
        else:
            dec_copy(other, me).wait_send()
        return 0

    lax.fori_loop(1, n, finish, 0)
    block_copy.wait()


def exchange(n, backward, *operands):
    share = ROWS // n
    outs = [jax.ShapeDtypeStruct((ROWS, LANES), BF16), jax.ShapeDtypeStruct((TOK, D), BF16)]
    if backward:
        outs.append(jax.ShapeDtypeStruct((n, INNER // n, 2 * TOK), BF16))
    else:
        outs.append(jax.ShapeDtypeStruct((n, 8, LANES), F32))
    dma = pltpu.SemaphoreType.DMA
    vmem = pl.BlockSpec(memory_space=pltpu.VMEM)
    return pl.pallas_call(
        functools.partial(exchange_kernel, n, backward),
        out_shape=outs,
        in_specs=[vmem] * len(operands),
        out_specs=[vmem] * 3,
        scratch_shapes=[
            pltpu.VMEM((n, share, LANES), BF16),
            pltpu.VMEM((n, share, LANES), BF16),
            dma((n,)), dma((n,)), dma((n,)), dma((n,)), dma, dma, dma((n,)), dma((n,)),
        ],
        compiler_params=pltpu.CompilerParams(
            collective_id=1 if backward else 0, has_side_effects=True, vmem_limit_bytes=VMEM_LIMIT
        ),
    )(*operands)


def strand_block(*shape):
    return pl.BlockSpec((1,) + shape, lambda s: (s,) + (0,) * len(shape))


def fixed_block(*shape):
    return pl.BlockSpec(shape, lambda s: (0,) * len(shape))


def out_of(*shape, dtype=BF16):
    return jax.ShapeDtypeStruct(shape, dtype)


PARAMS = pltpu.CompilerParams(vmem_limit_bytes=VMEM_LIMIT)


def cost(flops, count):
    return pl.CostEstimate(flops=flops, bytes_accessed=count, transcendentals=0)


def per_device(
    proj_main, proj_state, step_raw, step_bias, decay_log, skip_scale, norm_gain, out_weight, grad_mixed
):
    n = lax.axis_size("seq")
    share = ROWS // n
    spare = LANES - HEADS
    raw = jnp.pad(step_raw, ((0, 0), (0, 0), (0, spare)))
    bias, dlog, skip = (
        jnp.pad(v, (0, spare)).reshape(1, LANES) for v in (step_bias, decay_log, skip_scale)
    )
    gain = norm_gain.reshape(1, INNER)
    whole_weight = lax.all_gather(out_weight, "seq", axis=0, tiled=True)
    whole_grad = lax.all_gather(grad_mixed, "seq", axis=0, tiled=True)

    main_x = pl.BlockSpec((1, TOK, INNER), lambda s: (s, 0, 0))
    row = fixed_block(1, LANES)
    state_rows = HEADS * STATE
    st, dec = pl.pallas_call(
        local_state_kernel,
        grid=(2,),
        in_specs=[main_x, strand_block(TOK, 2 * STATE), strand_block(TOK, LANES), row, row],
        out_specs=[strand_block(state_rows, LANES), strand_block(1, LANES)],
        out_shape=[out_of(2, state_rows, LANES), out_of(2, 1, LANES, dtype=F32)],
        compiler_params=PARAMS,
    )(proj_main, proj_state, raw, bias, dlog)
    decays = dec[:, 0, :HEADS].reshape(2 * HEADS)
    table = [[min(j * share // STATE + k, 2 * HEADS - 1) for k in range(8)] for j in range(n)]
    decs = jnp.broadcast_to(decays[jnp.array(table)][:, :, None], (n, 8, LANES))
    entering, grad_far, decbox = exchange(n, False, st.reshape(ROWS, LANES), decs, grad_mixed)
    entering = entering.reshape(2, state_rows, LANES)

    nt, so, gz, gy, de, gyy = pl.pallas_call(
        middle_kernel,
        grid=(2,),
        in_specs=[
            strand_block(TOK, 2 * INNER), strand_block(TOK, 2 * STATE), strand_block(TOK, LANES),
            row, row, row, fixed_block(1, INNER), fixed_block(INNER, D), fixed_block(TOK, D),
            fixed_block(TOK, D), strand_block(state_rows, LANES),
        ],
        out_specs=[
            pl.BlockSpec((INNER, TOK), lambda s: (0, s)), strand_block(TOK, D),
            strand_block(TOK, INNER), strand_block(TOK, INNER), strand_block(state_rows, LANES),
            strand_block(TOK, LANES),
        ],
        out_shape=[
            out_of(INNER, 2 * TOK), out_of(2, TOK, D), out_of(2, TOK, INNER), out_of(2, TOK, INNER),
            out_of(2, state_rows, LANES), out_of(2, TOK, LANES, dtype=F32),
        ],
        scratch_shapes=[
            pltpu.VMEM((TOK, INNER), F32), pltpu.VMEM((TOK, INNER), F32),
            pltpu.VMEM((TOK, D), BF16), pltpu.VMEM((TOK, INNER), BF16),
        ],
        compiler_params=PARAMS,
    )(proj_main, proj_state, raw, bias, dlog, skip, gain, whole_weight, grad_mixed, grad_far, entering)

    leaving, so_far, all_nt = exchange(n, True, de.reshape(ROWS, LANES), decbox, so[1], nt)
    leaving = leaving.reshape(2, state_rows, LANES)

    grad_main, grad_state, grad_step = pl.pallas_call(
        last_kernel,
        grid=(2,),
        in_specs=[
            main_x, strand_block(TOK, INNER), strand_block(TOK, INNER), strand_block(TOK, 2 * STATE),
            strand_block(TOK, LANES), row, row, row, strand_block(state_rows, LANES),
            strand_block(state_rows, LANES), strand_block(TOK, LANES),
        ],
        out_specs=[strand_block(TOK, 2 * INNER), strand_block(TOK, 2 * STATE), strand_block(TOK, LANES)],
        out_shape=[
            out_of(2, TOK, 2 * INNER), out_of(2, TOK, 2 * STATE, dtype=F32), out_of(2, TOK, LANES, dtype=F32),
        ],
        scratch_shapes=[pltpu.VMEM((TOK, LANES), F32)],
        compiler_params=PARAMS,
    )(proj_main, gz, gy, proj_state, raw, bias, dlog, skip, entering, leaving, gyy)

    vmem = pl.BlockSpec(memory_space=pltpu.VMEM)
    grad_weight, mixed_out = pl.pallas_call(
        functools.partial(weight_kernel, n),
        in_specs=[vmem] * 4,
        out_specs=[vmem] * 2,
        out_shape=[out_of(INNER // n, D, dtype=F32), out_of(TOK, D)],
        compiler_params=PARAMS,
    )(all_nt, whole_grad, so[0], so_far)
    return mixed_out, grad_main, grad_state, grad_step[:, :, :HEADS], grad_weight


def solution(mesh):
    placed = (
        P(None, ("parts", "seq"), None), P(None, ("parts", "seq"), None),
        P(None, ("parts", "seq"), None), P(), P(), P(), P(), P("seq", None),
        P(("parts", "seq"), None),
    )
    return jax.shard_map(
        per_device,
        mesh=mesh,
        in_specs=placed,
        out_specs=(
            P(("parts", "seq"), None), P(None, ("parts", "seq"), None),
            P(None, ("parts", "seq"), None), P(None, ("parts", "seq"), None),
            P(("parts", "seq"), None),
        ),
        check_vma=False,
    )
```

```python
import functools

import jax
import jax.numpy as jnp
from jax import lax
from jax.experimental import pallas as pl
from jax.experimental.pallas import tpu as pltpu
from jax.sharding import PartitionSpec as P

D = 1024
HEADS = 16
HEAD_DIM = 128
STATE = 64
INNER = 2048
TOK = 128
LANES = 128
ROWS = 2 * HEADS * STATE
EPSILON = 1e-05
HIGH = lax.Precision.HIGHEST
F32 = jnp.float32
BF16 = jnp.bfloat16
MESH = pl.DeviceIdType.MESH
VMEM_LIMIT = 56 * 2**20


def dot(a, b, ca=1, cb=0, precision=None):
    return lax.dot_general(
        a, b, (((ca,), (cb,)), ((), ())), precision=precision, preferred_element_type=F32
    )


def grids(shape=(TOK, TOK)):
    return lax.broadcasted_iota(jnp.int32, shape, 0), lax.broadcasted_iota(jnp.int32, shape, 1)


def anti_identity():
    row, col = grids()
    return (row + col == TOK - 1).astype(BF16)


def flip_both(block):
    anti = anti_identity()
    turned = dot(anti, block).astype(BF16)
    count = block.shape[1] // TOK
    parts = [
        dot(turned[:, (count - 1 - k) * TOK : (count - k) * TOK], anti).astype(BF16)
        for k in range(count)
    ]
    return jnp.concatenate(parts, axis=1)


def steps(raw, bias, dlog):
    arg = raw + bias
    size = jnp.maximum(arg, 0.0) + jnp.log1p(jnp.exp(-jnp.abs(arg)))
    rate = -jnp.exp(dlog) * size
    row, col = grids()
    lower = (row >= col).astype(F32)
    cum = dot(lower, rate, precision=HIGH)
    return arg, size, rate, cum


def head(h):
    return slice(h * HEAD_DIM, (h + 1) * HEAD_DIM)


def srows(h):
    return slice(h * STATE, (h + 1) * STATE)


def local_state_kernel(x_ref, bc_ref, raw_ref, bias_ref, dlog_ref, st_ref, dec_ref):
    _, size, _, cum = steps(raw_ref[0], bias_ref[...], dlog_ref[...])
    total = cum[TOK - 1 : TOK, :]
    weight = jnp.exp(total - cum) * size
    b = bc_ref[0, :, :STATE]
    for h in range(HEADS):
        xw = (x_ref[0, :, head(h)].astype(F32) * weight[:, h : h + 1]).astype(BF16)
        st_ref[0, srows(h), :] = dot(b, xw, 0, 0).astype(BF16)
    dec_ref[0] = jnp.exp(total)


def mixing(scores, mask, cum, cum_t, size_t, h):
    gap = cum[:, h : h + 1] - cum_t[h : h + 1, :]
    decay = jnp.where(mask, jnp.exp(jnp.minimum(gap, 0.0)), 0.0)
    return decay * size_t[h : h + 1, :]


def middle_kernel(
    main_ref, bc_ref, raw_ref, bias_ref, dlog_ref, skip_ref, gain_ref, w_ref, gm_ref, gmm_ref, e_ref,
    nt_ref, so_ref, gz_ref, gy_ref, de_ref, gyy_ref,
    y_s, gn_s, bi_s, no_s,
):
    strand = pl.program_id(0)

    @pl.when(strand == 0)
    def _():
        bi_s[...] = gm_ref[...]

    @pl.when(strand == 1)
    def _():
        bi_s[...] = flip_both(gmm_ref[...])

    gn_s[...] = dot(bi_s[...], w_ref[...], 1, 1) * gain_ref[...]
    _, size, _, cum = steps(raw_ref[0], bias_ref[...], dlog_ref[...])
    cum_t, size_t = cum.T, size.T
    ecum = jnp.exp(cum)
    b, c = bc_ref[0, :, :STATE], bc_ref[0, :, STATE:]
    scores = dot(c, b, 1, 1)
    row, col = grids()
    mask = row >= col
    squares = jnp.zeros((TOK, LANES), F32)
    crossed = jnp.zeros((TOK, LANES), F32)
    for h in range(HEADS):
        m = (scores * mixing(scores, mask, cum, cum_t, size_t, h)).astype(BF16)
        x = main_ref[0, :, head(h)]
        y = dot(m, x) + ecum[:, h : h + 1] * dot(c, e_ref[0, srows(h), :])
        y = y + skip_ref[0:1, h : h + 1] * x.astype(F32)
        y_s[:, head(h)] = y
        z = main_ref[0, :, INNER + h * HEAD_DIM : INNER + (h + 1) * HEAD_DIM].astype(F32)
        gated = y * (z / (1.0 + jnp.exp(-z)))
        squares += gated * gated
        crossed += gated * gn_s[:, head(h)]
    r = lax.rsqrt(jnp.sum(squares, axis=1, keepdims=True) / INNER + EPSILON)
    factor = r * r * r * (jnp.sum(crossed, axis=1, keepdims=True) / INNER)
    spin = jnp.where(strand == 0, (row == col).astype(F32), (row + col == TOK - 1).astype(F32))
    spin = spin.astype(BF16)
    for h in range(HEADS):
        z = main_ref[0, :, INNER + h * HEAD_DIM : INNER + (h + 1) * HEAD_DIM].astype(F32)
        y = y_s[:, head(h)]
        sig = 1.0 / (1.0 + jnp.exp(-z))
        silu = z * sig
        gated = y * silu
        normed = (gated * r * gain_ref[:, head(h)]).astype(BF16)
        no_s[:, head(h)] = normed
        nt_ref[head(h), :] = dot(normed, spin, 0, 0).astype(BF16)
        dgated = r * gn_s[:, head(h)] - gated * factor
        gz_ref[0, :, head(h)] = (dgated * y * (sig * (1.0 + z * (1.0 - sig)))).astype(BF16)
        gy = (dgated * silu).astype(BF16)
        gy_ref[0, :, head(h)] = gy
        gyf = gy.astype(F32)
        scan_y = y - skip_ref[0:1, h : h + 1] * main_ref[0, :, head(h)].astype(F32)
        gyy_ref[0, :, h : h + 1] = jnp.sum(gyf * scan_y, axis=1, keepdims=True)
        de_ref[0, srows(h), :] = dot(c, (gyf * ecum[:, h : h + 1]).astype(BF16), 0, 0).astype(BF16)
    so_ref[0] = dot(no_s[...], w_ref[...]).astype(BF16)


def last_kernel(
    x_ref, gz_ref, gy_ref, bc_ref, raw_ref, bias_ref, dlog_ref, skip_ref, e_ref, lv_ref, gyy_ref,
    gmain_ref, gstate_ref, gstep_ref,
    xdx_s,
):
    arg, size, _, cum = steps(raw_ref[0], bias_ref[...], dlog_ref[...])
    cum_t, size_t = cum.T, size.T
    ecum = jnp.exp(cum)
    total = cum[TOK - 1 : TOK, :]
    weight = jnp.exp(total - cum) * size
    b, c = bc_ref[0, :, :STATE], bc_ref[0, :, STATE:]
    scores = dot(c, b, 1, 1)
    row, col = grids()
    mask = row >= col
    lane = lax.broadcasted_iota(jnp.int32, (1, LANES), 1)
    gscore = jnp.zeros((TOK, TOK), F32)
    gb = jnp.zeros((TOK, STATE), F32)
    gc = jnp.zeros((TOK, STATE), F32)
    gtotal = jnp.zeros((1, LANES), F32)
    xdx_s[...] = jnp.zeros_like(xdx_s)
    for h in range(HEADS):
        w = mixing(scores, mask, cum, cum_t, size_t, h)
        m = (scores * w).astype(BF16)
        x, gy = x_ref[0, :, head(h)], gy_ref[0, :, head(h)]
        xf, gyf = x.astype(F32), gy.astype(F32)
        lv, e = lv_ref[0, srows(h), :], e_ref[0, srows(h), :]
        gscore += dot(gy, x, 1, 1) * w
        wcol = weight[:, h : h + 1]
        through = wcol * dot(b, lv)
        dx = dot(m, gy, 0, 0) + through
        gmain_ref[0, :, head(h)] = (dx + skip_ref[0:1, h : h + 1] * gyf).astype(BF16)
        xdx_s[:, h : h + 1] = jnp.sum(xf * dx, axis=1, keepdims=True)
        gc += dot((gyf * ecum[:, h : h + 1]).astype(BF16), e, 1, 1)
        gb += dot((xf * wcol).astype(BF16), lv, 1, 1)
        held = jnp.sum(xf * through, axis=0, keepdims=True)
        kept = jnp.sum(e.astype(F32) * lv.astype(F32), axis=0, keepdims=True)
        both = jnp.sum(held + jnp.exp(total[:, h : h + 1]) * kept, axis=1, keepdims=True)
        gtotal += jnp.where(lane == h, both, 0.0)
    gs = gscore.astype(BF16)
    gstate_ref[0, :, :STATE] = gb + dot(gs, c, 0, 0)
    gstate_ref[0, :, STATE:] = gc + dot(gs, b)
    gmain_ref[0, :, INNER:] = gz_ref[0]
    real = lane < HEADS
    gcum = jnp.where(real, gyy_ref[0], 0.0) - xdx_s[...]
    upper = (row <= col).astype(F32)
    grate = dot(upper, gcum, precision=HIGH) + gtotal
    gsize = xdx_s[...] / size - jnp.exp(dlog_ref[...]) * grate
    gstep_ref[0] = gsize / (1.0 + jnp.exp(-arg))


def weight_kernel(n, nt_ref, gm_ref, so_ref, som_ref, gw_ref, mixed_ref):
    plain = jnp.zeros(gw_ref.shape, F32)
    turned = jnp.zeros(gw_ref.shape, F32)

    def body(i, held):
        plain, turned = held
        near = gm_ref[pl.ds(pl.multiple_of(i * TOK, TOK), TOK), :]
        far = gm_ref[pl.ds(pl.multiple_of((n - 1 - i) * TOK, TOK), TOK), :]
        return plain + dot(nt_ref[i, :, :TOK], near), turned + dot(nt_ref[i, :, TOK:], far)

    plain, turned = lax.fori_loop(0, n, body, (plain, turned))
    row, col = grids()
    anti = (row + col == TOK - 1).astype(F32)
    count = D // TOK
    for k in range(count):
        back = turned[:, (count - 1 - k) * TOK : (count - k) * TOK]
        gw_ref[:, k * TOK : (k + 1) * TOK] = plain[:, k * TOK : (k + 1) * TOK] + dot(
            back, anti, precision=HIGH
        )
    mixed_ref[...] = (so_ref[...].astype(F32) + flip_both(som_ref[...]).astype(F32)).astype(BF16)


def exchange_kernel(n, backward, *refs):
    if backward:
        (st_ref, dec_ref, block_ref, matedec, decbox, nt_ref, out_ref, gotblock_ref, gotnt_ref) = refs[:9]
        rest = refs[9:]
    else:
        (st_ref, dec_ref, block_ref, w_ref, out_ref, gotblock_ref, matedec, decbox, wall_ref) = refs[:9]
        rest = refs[9:]
    (mate, comb, inbox, outbox, fbox, other, decout), sems = rest[:7], rest[7:]
    (mate_send, mate_recv, in_send, in_recv, f_send, f_recv, last_send, last_recv, block_send, block_recv) = sems[:10]
    extra = sems[10:]
    me = lax.axis_index("seq")
    chips = n // 2
    chip, core = me // 2, lax.rem(me, 2)
    partner = me + 1 - 2 * core
    half = ROWS // 2
    share = half // chips
    inner = INNER // n
    groups = max(1, share // STATE)
    size = share // groups
    barrier = pltpu.get_barrier_semaphore()

    def greet(k, _):
        pl.semaphore_signal(
            barrier, inc=1, device_id={"seq": lax.rem(me + k, n)}, device_id_type=MESH
        )
        return 0

    lax.fori_loop(1, n, greet, 0)
    pl.semaphore_wait(barrier, n - 1)

    def rows_of(i, count):
        return pl.ds(pl.multiple_of(i * count, count), count)

    def remote(src, dst, send, recv, to):
        return pltpu.make_async_remote_copy(
            src_ref=src, dst_ref=dst, send_sem=send, recv_sem=recv,
            device_id={"seq": to}, device_id_type=MESH,
        )

    to_mate = remote(st_ref.at[rows_of(1 - core, half), :], mate, mate_send.at[0], mate_recv.at[0], partner)
    to_mate.start()
    dec_mate = None
    if not backward:
        dec_mate = remote(dec_ref.at[rows_of(1 - core, HEADS), :], matedec, mate_send.at[1], mate_recv.at[1], partner)
        dec_mate.start()

    def in_copy(to, slot):
        return remote(
            comb.at[rows_of(to, share), :], inbox.at[slot], in_send.at[to], in_recv.at[slot], 2 * to + core
        )

    def dec_copy(to, slot):
        return remote(decout.at[to], decbox.at[slot], extra[0].at[to], extra[1].at[slot], 2 * to + core)

    def f_copy(to, slot):
        return remote(
            outbox.at[to], fbox.at[rows_of(slot, share), :], f_send.at[to], f_recv.at[slot], 2 * to + core
        )

    def nt_copy(to, slot):
        return remote(
            nt_ref.at[rows_of(to, inner), :], gotnt_ref.at[slot], extra[0].at[to], extra[1].at[slot], to
        )

    block_copy = remote(block_ref, gotblock_ref, block_send, block_recv, n - 1 - me)

    if not backward:
        w_recv, cw_send, ccw_send, pair_send = extra[2:]
        place = jnp.where(lax.rem(chip, 2) == 0, chip // 2, chips - 1 - chip // 2)

        def at(offset):
            pos = lax.rem(place + offset + 2 * chips, chips)
            return jnp.where(pos < chips // 2, 2 * pos, 2 * (chips - 1 - pos) + 1)

        def w_copy(block, sems_, to):
            return remote(wall_ref.at[block], wall_ref.at[block], sems_.at[block], w_recv.at[block], to)

        right, left = 2 * at(1) + core, 2 * at(-1) + core
        cw_steps = chips // 2
        ccw_steps = chips - 1 - cw_steps
        sent = []

        def launch(copy):
            copy.start()
            sent.append(copy)

        def ring(step):
            if step < cw_steps:
                block = 2 * at(-step) + core
                if step > 0:
                    w_copy(block, cw_send, right).wait_recv()
                launch(w_copy(block, cw_send, right))
                if step > 0:
                    launch(w_copy(block, pair_send, partner))
            if step < ccw_steps:
                block = 2 * at(step) + core
                if step > 0:
                    w_copy(block, ccw_send, left).wait_recv()
                launch(w_copy(block, ccw_send, left))
                launch(w_copy(block, pair_send, partner))
            if step == cw_steps:
                block = 2 * at(-step) + core
                w_copy(block, cw_send, right).wait_recv()
                launch(w_copy(block, pair_send, partner))
            if step == ccw_steps:
                block = 2 * at(step) + core
                w_copy(block, ccw_send, left).wait_recv()
                launch(w_copy(block, pair_send, partner))

        wall_ref[me] = w_ref[...]
        ring(0)

    def scaled(dec, rows, h):
        return dec[h : h + 1, :] * rows.astype(F32)

    near_is_me = core == (1 if backward else 0)
    to_mate.wait_recv()
    if not backward:
        dec_mate.wait_recv()
    mydec = dec_ref[rows_of(core, HEADS), :]
    itsdec = matedec[...]
    neardec = jnp.where(near_is_me, mydec, itsdec)
    fardec = jnp.where(near_is_me, itsdec, mydec)
    for h in range(HEADS):
        mine = st_ref[pl.ds(pl.multiple_of(core * half + h * STATE, STATE), STATE), :]
        its = mate[srows(h), :]
        near = jnp.where(near_is_me, mine.astype(F32), its.astype(F32))
        far = jnp.where(near_is_me, its.astype(F32), mine.astype(F32))
        comb[srows(h), :] = (scaled(fardec, near, h) + far).astype(BF16)
    if not backward:
        both = neardec * fardec
        for j in range(chips):
            first = j * share // STATE
            decout[j, :groups, :] = both[first : first + groups, :]

    def start_in(k, _):
        to = lax.rem(chip + k, chips)
        if not backward:
            dec_copy(to, chip).start()
        in_copy(to, chip).start()
        return 0

    lax.fori_loop(1, chips, start_in, 0)
    block_copy.start()
    inbox[chip] = comb[rows_of(chip, share), :]
    if backward:
        lax.fori_loop(1, n, lambda k, _: (nt_copy(lax.rem(me + k, n), me).start(), 0)[1], 0)
        gotnt_ref[me] = nt_ref[rows_of(me, inner), :]
    else:
        decbox[chip] = decout[chip]

    def arrive(k, _):
        peer = lax.rem(chip + k, chips)
        if not backward:
            dec_copy(peer, peer).wait_recv()
        in_copy(peer, peer).wait_recv()
        return 0

    lax.fori_loop(1, chips, arrive, 0)

    def scan(k, held):
        i = chips - 1 - k if backward else k
        outbox[i] = held.astype(BF16)

        @pl.when(i != chip)
        def _():
            f_copy(i, chip).start()

        grown = [
            held[g * size : (g + 1) * size] * decbox[i, g : g + 1, :] for g in range(groups)
        ]
        grown = grown[0] if groups == 1 else jnp.concatenate(grown, axis=0)
        return grown + inbox[i].astype(F32)

    lax.fori_loop(0, chips, scan, jnp.zeros((share, LANES), F32))
    fbox[rows_of(chip, share), :] = outbox[chip]
    if not backward:
        ring(1)

    def landed(k, _):
        peer = lax.rem(chip + k, chips)
        f_copy(peer, peer).wait_recv()
        return 0

    lax.fori_loop(1, chips, landed, 0)
    for h in range(HEADS):
        rows = pl.ds(pl.multiple_of(core * half + h * STATE, STATE), STATE)
        came = fbox[srows(h), :].astype(F32)
        near = jnp.where(near_is_me, st_ref[rows, :].astype(F32), mate[srows(h), :].astype(F32))
        later = scaled(neardec, came, h) + near
        out_ref[rows, :] = jnp.where(near_is_me, came, later).astype(BF16)
        other[srows(h), :] = jnp.where(near_is_me, later, came).astype(BF16)
    last = remote(other, out_ref.at[rows_of(core, half), :], last_send, last_recv, partner)
    last.start()
    if not backward:
        for step in range(2, cw_steps + 1):
            ring(step)

        def mate_block(k, _):
            block = 2 * k + 1 - core
            w_copy(block, pair_send, partner).wait_recv()
            return 0

        lax.fori_loop(0, chips, mate_block, 0)
        for copy in sent:
            copy.wait_send()
        dec_mate.wait_send()

    def finish(k, _):
        peer = lax.rem(chip + k, chips)
        in_copy(peer, chip).wait_send()
        f_copy(peer, chip).wait_send()
        if not backward:
            dec_copy(peer, chip).wait_send()
        return 0

    lax.fori_loop(1, chips, finish, 0)
    if backward:

        def finish_nt(k, _):
            peer = lax.rem(me + k, n)
            nt_copy(peer, peer).wait_recv()
            nt_copy(peer, me).wait_send()
            return 0

        lax.fori_loop(1, n, finish_nt, 0)
    to_mate.wait_send()
    last.wait()
    block_copy.wait()


def exchange(n, backward, *operands):
    chips = n // 2
    share = ROWS // n
    outs = [out_of(ROWS, LANES), out_of(TOK, D)]
    if backward:
        outs.append(out_of(n, INNER // n, 2 * TOK))
    else:
        outs += [
            out_of(HEADS, LANES, dtype=F32), out_of(chips, 8, LANES, dtype=F32), out_of(n, INNER // n, D)
        ]
    dma = pltpu.SemaphoreType.DMA
    vmem = pl.BlockSpec(memory_space=pltpu.VMEM)
    sems = [dma((2,)), dma((2,)), dma((chips,)), dma((chips,)), dma((chips,)), dma((chips,)), dma, dma, dma, dma]
    if backward:
        sems += [dma((n,)), dma((n,))]
    else:
        sems += [dma((chips,)), dma((chips,)), dma((n,)), dma((n,)), dma((n,)), dma((n,))]
    return pl.pallas_call(
        functools.partial(exchange_kernel, n, backward),
        out_shape=outs,
        in_specs=[vmem] * len(operands),
        out_specs=[vmem] * len(outs),
        scratch_shapes=[
            pltpu.VMEM((ROWS // 2, LANES), BF16), pltpu.VMEM((ROWS // 2, LANES), BF16),
            pltpu.VMEM((chips, share, LANES), BF16), pltpu.VMEM((chips, share, LANES), BF16),
            pltpu.VMEM((ROWS // 2, LANES), BF16), pltpu.VMEM((ROWS // 2, LANES), BF16),
            pltpu.VMEM((chips, 8, LANES), F32),
        ] + sems,
        compiler_params=pltpu.CompilerParams(
            collective_id=1 if backward else 0, has_side_effects=True, vmem_limit_bytes=VMEM_LIMIT
        ),
    )(*operands)


def strand_block(*shape):
    return pl.BlockSpec((1,) + shape, lambda s: (s,) + (0,) * len(shape))


def fixed_block(*shape):
    return pl.BlockSpec(shape, lambda s: (0,) * len(shape))


def out_of(*shape, dtype=BF16):
    return jax.ShapeDtypeStruct(shape, dtype)


PARAMS = pltpu.CompilerParams(vmem_limit_bytes=VMEM_LIMIT)


def cost(flops, count):
    return pl.CostEstimate(flops=flops, bytes_accessed=count, transcendentals=0)


def per_device(
    proj_main, proj_state, step_raw, step_bias, decay_log, skip_scale, norm_gain, out_weight, grad_mixed
):
    n = lax.axis_size("seq")
    spare = LANES - HEADS
    raw = jnp.pad(step_raw, ((0, 0), (0, 0), (0, spare)))
    bias, dlog, skip = (
        jnp.pad(v, (0, spare)).reshape(1, LANES) for v in (step_bias, decay_log, skip_scale)
    )
    gain = norm_gain.reshape(1, INNER)
    whole_grad = lax.all_gather(grad_mixed, "seq", axis=0, tiled=True)

    main_x = pl.BlockSpec((1, TOK, INNER), lambda s: (s, 0, 0))
    row = fixed_block(1, LANES)
    state_rows = HEADS * STATE
    st, dec = pl.pallas_call(
        local_state_kernel,
        grid=(2,),
        in_specs=[main_x, strand_block(TOK, 2 * STATE), strand_block(TOK, LANES), row, row],
        out_specs=[strand_block(state_rows, LANES), strand_block(1, LANES)],
        out_shape=[out_of(2, state_rows, LANES), out_of(2, 1, LANES, dtype=F32)],
        compiler_params=PARAMS,
    )(proj_main, proj_state, raw, bias, dlog)
    decs = jnp.broadcast_to(dec[:, 0, :HEADS, None], (2, HEADS, LANES)).reshape(2 * HEADS, LANES)
    entering, grad_far, matedec, decbox, whole_weight = exchange(
        n, False, st.reshape(ROWS, LANES), decs, grad_mixed, out_weight
    )
    whole_weight = whole_weight.reshape(INNER, D)
    entering = entering.reshape(2, state_rows, LANES)

    nt, so, gz, gy, de, gyy = pl.pallas_call(
        middle_kernel,
        grid=(2,),
        in_specs=[
            strand_block(TOK, 2 * INNER), strand_block(TOK, 2 * STATE), strand_block(TOK, LANES),
            row, row, row, fixed_block(1, INNER), fixed_block(INNER, D), fixed_block(TOK, D),
            fixed_block(TOK, D), strand_block(state_rows, LANES),
        ],
        out_specs=[
            pl.BlockSpec((INNER, TOK), lambda s: (0, s)), strand_block(TOK, D),
            strand_block(TOK, INNER), strand_block(TOK, INNER), strand_block(state_rows, LANES),
            strand_block(TOK, LANES),
        ],
        out_shape=[
            out_of(INNER, 2 * TOK), out_of(2, TOK, D), out_of(2, TOK, INNER), out_of(2, TOK, INNER),
            out_of(2, state_rows, LANES), out_of(2, TOK, LANES, dtype=F32),
        ],
        scratch_shapes=[
            pltpu.VMEM((TOK, INNER), F32), pltpu.VMEM((TOK, INNER), F32),
            pltpu.VMEM((TOK, D), BF16), pltpu.VMEM((TOK, INNER), BF16),
        ],
        compiler_params=PARAMS,
    )(proj_main, proj_state, raw, bias, dlog, skip, gain, whole_weight, grad_mixed, grad_far, entering)

    leaving, so_far, all_nt = exchange(
        n, True, de.reshape(ROWS, LANES), decs, so[1], matedec, decbox, nt
    )
    leaving = leaving.reshape(2, state_rows, LANES)

    grad_main, grad_state, grad_step = pl.pallas_call(
        last_kernel,
        grid=(2,),
        in_specs=[
            main_x, strand_block(TOK, INNER), strand_block(TOK, INNER), strand_block(TOK, 2 * STATE),
            strand_block(TOK, LANES), row, row, row, strand_block(state_rows, LANES),
            strand_block(state_rows, LANES), strand_block(TOK, LANES),
        ],
        out_specs=[strand_block(TOK, 2 * INNER), strand_block(TOK, 2 * STATE), strand_block(TOK, LANES)],
        out_shape=[
            out_of(2, TOK, 2 * INNER), out_of(2, TOK, 2 * STATE, dtype=F32), out_of(2, TOK, LANES, dtype=F32),
        ],
        scratch_shapes=[pltpu.VMEM((TOK, LANES), F32)],
        compiler_params=PARAMS,
    )(proj_main, gz, gy, proj_state, raw, bias, dlog, skip, entering, leaving, gyy)

    vmem = pl.BlockSpec(memory_space=pltpu.VMEM)
    grad_weight, mixed_out = pl.pallas_call(
        functools.partial(weight_kernel, n),
        in_specs=[vmem] * 4,
        out_specs=[vmem] * 2,
        out_shape=[out_of(INNER // n, D, dtype=F32), out_of(TOK, D)],
        compiler_params=PARAMS,
    )(all_nt, whole_grad, so[0], so_far)
    return mixed_out, grad_main, grad_state, grad_step[:, :, :HEADS], grad_weight


def solution(mesh):
    placed = (
        P(None, ("parts", "seq"), None), P(None, ("parts", "seq"), None),
        P(None, ("parts", "seq"), None), P(), P(), P(), P(), P("seq", None),
        P(("parts", "seq"), None),
    )
    return jax.shard_map(
        per_device,
        mesh=mesh,
        in_specs=placed,
        out_specs=(
            P(("parts", "seq"), None), P(None, ("parts", "seq"), None),
            P(None, ("parts", "seq"), None), P(None, ("parts", "seq"), None),
            P(("parts", "seq"), None),
        ),
        check_vma=False,
    )
```

```python
import functools

import jax
import jax.numpy as jnp
from jax import lax
from jax.experimental import pallas as pl
from jax.experimental.pallas import tpu as pltpu
from jax.sharding import PartitionSpec as P

D = 1024
HEADS = 16
HEAD_DIM = 128
STATE = 64
INNER = 2048
TOK = 128
LANES = 128
ROWS = 2 * HEADS * STATE
EPSILON = 1e-05
HIGH = lax.Precision.HIGHEST
F32 = jnp.float32
BF16 = jnp.bfloat16
MESH = pl.DeviceIdType.MESH
VMEM_LIMIT = 56 * 2**20


def dot(a, b, ca=1, cb=0, precision=None):
    return lax.dot_general(
        a, b, (((ca,), (cb,)), ((), ())), precision=precision, preferred_element_type=F32
    )


def grids(shape=(TOK, TOK)):
    return lax.broadcasted_iota(jnp.int32, shape, 0), lax.broadcasted_iota(jnp.int32, shape, 1)


def anti_identity():
    row, col = grids()
    return (row + col == TOK - 1).astype(BF16)


def flip_both(block):
    anti = anti_identity()
    turned = dot(anti, block).astype(BF16)
    count = block.shape[1] // TOK
    parts = [
        dot(turned[:, (count - 1 - k) * TOK : (count - k) * TOK], anti).astype(BF16)
        for k in range(count)
    ]
    return jnp.concatenate(parts, axis=1)


def steps(raw_t, bias, dlog):
    raw = jnp.concatenate([raw_t, jnp.zeros((LANES - HEADS, TOK), F32)], axis=0).T
    arg = raw + bias
    size = jnp.maximum(arg, 0.0) + jnp.log1p(jnp.exp(-jnp.abs(arg)))
    rate = -jnp.exp(dlog) * size
    row, col = grids()
    lower = (row >= col).astype(F32)
    cum = dot(lower, rate, precision=HIGH)
    return arg, size, rate, cum


def head(h):
    return slice(h * HEAD_DIM, (h + 1) * HEAD_DIM)


def srows(h):
    return slice(h * STATE, (h + 1) * STATE)


def local_state_kernel(x_ref, bc_ref, raw_ref, bias_ref, dlog_ref, st_ref, dec_ref):
    _, size, _, cum = steps(raw_ref[0], bias_ref[...], dlog_ref[...])
    total = cum[TOK - 1 : TOK, :]
    weight = jnp.exp(total - cum) * size
    b = bc_ref[0, :, :STATE]
    for h in range(HEADS):
        xw = (x_ref[0, :, head(h)].astype(F32) * weight[:, h : h + 1]).astype(BF16)
        st_ref[0, srows(h), :] = dot(b, xw, 0, 0).astype(BF16)
    dec_ref[0] = jnp.broadcast_to(jnp.exp(cum.T[:HEADS, TOK - 1 :]), (HEADS, LANES))


def mixing(scores, mask, cum, cum_t, size_t, h):
    gap = cum[:, h : h + 1] - cum_t[h : h + 1, :]
    decay = jnp.where(mask, jnp.exp(jnp.minimum(gap, 0.0)), 0.0)
    return decay * size_t[h : h + 1, :]


def middle_kernel(
    main_ref, bc_ref, raw_ref, bias_ref, dlog_ref, skip_ref, gain_ref, w_ref, gm_ref, gmm_ref, e_ref,
    nt_ref, so_ref, gz_ref, gy_ref, de_ref, gyy_ref,
    y_s, gn_s, bi_s, no_s,
):
    strand = pl.program_id(0)

    @pl.when(strand == 0)
    def _():
        bi_s[...] = gm_ref[...]

    @pl.when(strand == 1)
    def _():
        bi_s[...] = flip_both(gmm_ref[...])

    gn_s[...] = dot(bi_s[...], w_ref[...], 1, 1) * gain_ref[...]
    _, size, _, cum = steps(raw_ref[0], bias_ref[...], dlog_ref[...])
    cum_t, size_t = cum.T, size.T
    ecum = jnp.exp(cum)
    b, c = bc_ref[0, :, :STATE], bc_ref[0, :, STATE:]
    scores = dot(c, b, 1, 1)
    row, col = grids()
    mask = row >= col
    squares = jnp.zeros((TOK, LANES), F32)
    crossed = jnp.zeros((TOK, LANES), F32)
    for h in range(HEADS):
        m = (scores * mixing(scores, mask, cum, cum_t, size_t, h)).astype(BF16)
        x = main_ref[0, :, head(h)]
        y = dot(m, x) + ecum[:, h : h + 1] * dot(c, e_ref[0, srows(h), :])
        y = y + skip_ref[0:1, h : h + 1] * x.astype(F32)
        y_s[:, head(h)] = y
        z = main_ref[0, :, INNER + h * HEAD_DIM : INNER + (h + 1) * HEAD_DIM].astype(F32)
        gated = y * (z / (1.0 + jnp.exp(-z)))
        squares += gated * gated
        crossed += gated * gn_s[:, head(h)]
    r = lax.rsqrt(jnp.sum(squares, axis=1, keepdims=True) / INNER + EPSILON)
    factor = r * r * r * (jnp.sum(crossed, axis=1, keepdims=True) / INNER)
    spin = jnp.where(strand == 0, (row == col).astype(F32), (row + col == TOK - 1).astype(F32))
    spin = spin.astype(BF16)
    for h in range(HEADS):
        z = main_ref[0, :, INNER + h * HEAD_DIM : INNER + (h + 1) * HEAD_DIM].astype(F32)
        y = y_s[:, head(h)]
        sig = 1.0 / (1.0 + jnp.exp(-z))
        silu = z * sig
        gated = y * silu
        normed = (gated * r * gain_ref[:, head(h)]).astype(BF16)
        no_s[:, head(h)] = normed
        nt_ref[head(h), :] = dot(normed, spin, 0, 0).astype(BF16)
        dgated = r * gn_s[:, head(h)] - gated * factor
        gz_ref[0, :, head(h)] = (dgated * y * (sig * (1.0 + z * (1.0 - sig)))).astype(BF16)
        gy = (dgated * silu).astype(BF16)
        gy_ref[0, :, head(h)] = gy
        gyf = gy.astype(F32)
        scan_y = y - skip_ref[0:1, h : h + 1] * main_ref[0, :, head(h)].astype(F32)
        gyy_ref[0, :, h : h + 1] = jnp.sum(gyf * scan_y, axis=1, keepdims=True)
        de_ref[0, srows(h), :] = dot(c, (gyf * ecum[:, h : h + 1]).astype(BF16), 0, 0).astype(BF16)
    so_ref[0] = dot(no_s[...], w_ref[...]).astype(BF16)


def last_kernel(
    x_ref, gz_ref, gy_ref, bc_ref, raw_ref, bias_ref, dlog_ref, skip_ref, e_ref, lv_ref, gyy_ref,
    gmain_ref, gstate_ref, gstep_ref,
    xdx_s,
):
    arg, size, _, cum = steps(raw_ref[0], bias_ref[...], dlog_ref[...])
    cum_t, size_t = cum.T, size.T
    ecum = jnp.exp(cum)
    total = cum[TOK - 1 : TOK, :]
    weight = jnp.exp(total - cum) * size
    b, c = bc_ref[0, :, :STATE], bc_ref[0, :, STATE:]
    scores = dot(c, b, 1, 1)
    row, col = grids()
    mask = row >= col
    lane = lax.broadcasted_iota(jnp.int32, (1, LANES), 1)
    gscore = jnp.zeros((TOK, TOK), F32)
    gb = jnp.zeros((TOK, STATE), F32)
    gc = jnp.zeros((TOK, STATE), F32)
    gtotal = jnp.zeros((1, LANES), F32)
    xdx_s[...] = jnp.zeros_like(xdx_s)
    for h in range(HEADS):
        w = mixing(scores, mask, cum, cum_t, size_t, h)
        m = (scores * w).astype(BF16)
        x, gy = x_ref[0, :, head(h)], gy_ref[0, :, head(h)]
        xf, gyf = x.astype(F32), gy.astype(F32)
        lv, e = lv_ref[0, srows(h), :], e_ref[0, srows(h), :]
        gscore += dot(gy, x, 1, 1) * w
        wcol = weight[:, h : h + 1]
        through = wcol * dot(b, lv)
        dx = dot(m, gy, 0, 0) + through
        gmain_ref[0, :, head(h)] = (dx + skip_ref[0:1, h : h + 1] * gyf).astype(BF16)
        xdx_s[:, h : h + 1] = jnp.sum(xf * dx, axis=1, keepdims=True)
        gc += dot((gyf * ecum[:, h : h + 1]).astype(BF16), e, 1, 1)
        gb += dot((xf * wcol).astype(BF16), lv, 1, 1)
        held = jnp.sum(xf * through, axis=0, keepdims=True)
        kept = jnp.sum(e.astype(F32) * lv.astype(F32), axis=0, keepdims=True)
        both = jnp.sum(held + jnp.exp(total[:, h : h + 1]) * kept, axis=1, keepdims=True)
        gtotal += jnp.where(lane == h, both, 0.0)
    gs = gscore.astype(BF16)
    gstate_ref[0, :, :STATE] = gb + dot(gs, c, 0, 0)
    gstate_ref[0, :, STATE:] = gc + dot(gs, b)
    gmain_ref[0, :, INNER:] = gz_ref[0]
    real = lane < HEADS
    gcum = jnp.where(real, gyy_ref[0], 0.0) - xdx_s[...]
    upper = (row <= col).astype(F32)
    grate = dot(upper, gcum, precision=HIGH) + gtotal
    gsize = xdx_s[...] / size - jnp.exp(dlog_ref[...]) * grate
    gstep_ref[0] = (gsize / (1.0 + jnp.exp(-arg))).T[:HEADS]


def weight_kernel(n, nt_ref, gm_ref, so_ref, som_ref, gw_ref, mixed_ref):
    near = jnp.concatenate([nt_ref[i, :, :TOK] for i in range(n)], axis=1)
    far = jnp.concatenate([nt_ref[n - 1 - i, :, TOK:] for i in range(n)], axis=1)
    plain = dot(near, gm_ref[...])
    turned = dot(far, gm_ref[...])
    row, col = grids()
    anti = (row + col == TOK - 1).astype(F32)
    count = D // TOK
    for k in range(count):
        back = turned[:, (count - 1 - k) * TOK : (count - k) * TOK]
        gw_ref[:, k * TOK : (k + 1) * TOK] = plain[:, k * TOK : (k + 1) * TOK] + dot(
            back, anti, precision=HIGH
        )
    mixed_ref[...] = (so_ref[0].astype(F32) + flip_both(som_ref[...]).astype(F32)).astype(BF16)


def exchange_kernel(n, backward, *refs):
    if backward:
        (st_ref, dec_ref, block_ref, matedec, decbox, nt_ref, out_ref, gotblock_ref, gotnt_ref) = refs[:9]
        rest = refs[9:]
    else:
        (st_ref, dec_ref, g_ref, w_ref, out_ref, gall_ref, matedec, decbox, wall_ref) = refs[:9]
        rest = refs[9:]
    (mate, comb, inbox, outbox, fbox, other, decout), sems = rest[:7], rest[7:]
    (mate_send, mate_recv, in_send, in_recv, f_send, f_recv, last_send, last_recv, block_send, block_recv) = sems[:10]
    extra = sems[10:]
    me = lax.axis_index("seq")
    chips = n // 2
    chip, core = me // 2, lax.rem(me, 2)
    partner = me + 1 - 2 * core
    half = ROWS // 2
    share = half // chips
    inner = INNER // n
    groups = max(1, share // STATE)
    size = share // groups
    barrier = pltpu.get_barrier_semaphore()

    def greet(k, _):
        pl.semaphore_signal(
            barrier, inc=1, device_id={"seq": lax.rem(me + k, n)}, device_id_type=MESH
        )
        return 0

    lax.fori_loop(1, n, greet, 0)
    pl.semaphore_wait(barrier, n - 1)

    def rows_of(i, count):
        return pl.ds(pl.multiple_of(i * count, count), count)

    def remote(src, dst, send, recv, to):
        return pltpu.make_async_remote_copy(
            src_ref=src, dst_ref=dst, send_sem=send, recv_sem=recv,
            device_id={"seq": to}, device_id_type=MESH,
        )

    to_mate = remote(st_ref.at[rows_of(1 - core, half), :], mate, mate_send.at[0], mate_recv.at[0], partner)
    to_mate.start()
    dec_mate = None
    if not backward:
        dec_mate = remote(dec_ref.at[rows_of(1 - core, HEADS), :], matedec, mate_send.at[1], mate_recv.at[1], partner)
        dec_mate.start()

    def in_copy(to, slot):
        return remote(
            comb.at[rows_of(to, share), :], inbox.at[slot], in_send.at[to], in_recv.at[slot], 2 * to + core
        )

    def dec_copy(to, slot):
        return remote(decout.at[to], decbox.at[slot], extra[0].at[to], extra[1].at[slot], 2 * to + core)

    def f_copy(to, slot):
        return remote(
            outbox.at[to], fbox.at[rows_of(slot, share), :], f_send.at[to], f_recv.at[slot], 2 * to + core
        )

    def nt_copy(to, slot):
        return remote(
            nt_ref.at[rows_of(to, inner), :], gotnt_ref.at[slot], extra[0].at[to], extra[1].at[slot], to
        )

    if backward:
        block_copy = remote(block_ref.at[1], gotblock_ref, block_send, block_recv, n - 1 - me)

    if not backward:
        place = jnp.where(lax.rem(chip, 2) == 0, chip // 2, chips - 1 - chip // 2)

        def at(offset):
            pos = lax.rem(place + offset + 2 * chips, chips)
            return jnp.where(pos < chips // 2, 2 * pos, 2 * (chips - 1 - pos) + 1)

        right, left = 2 * at(1) + core, 2 * at(-1) + core
        cw_steps = chips // 2
        ccw_steps = chips - 1 - cw_steps
        sent = []

        def launch(copy):
            copy.start()
            sent.append(copy)

        def block_copy_of(which, block, lane, to):
            whole, sems_ = ((wall_ref, extra[2:6]), (gall_ref, extra[6:10]))[which]
            return remote(whole.at[block], whole.at[block], sems_[lane].at[block], sems_[3].at[block], to)

        def ring_of(which, step):
            for lane, count, sign, to in ((0, cw_steps, -1, right), (1, ccw_steps, 1, left)):
                if step > count:
                    continue
                block = 2 * at(sign * step) + core
                if step > 0:
                    block_copy_of(which, block, lane, to).wait_recv()
                if step < count:
                    launch(block_copy_of(which, block, lane, to))
                if step > 0 or lane == 0:
                    launch(block_copy_of(which, block, 2, partner))

        def ring(step):
            ring_of(0, step)
            ring_of(1, step)

        wall_ref[me] = w_ref[...]
        gall_ref[me] = g_ref[...]
        ring(0)

    def scaled(dec, rows, h):
        return dec[h : h + 1, :] * rows.astype(F32)

    near_is_me = core == (1 if backward else 0)
    to_mate.wait_recv()
    if not backward:
        dec_mate.wait_recv()
    mydec = dec_ref[rows_of(core, HEADS), :]
    itsdec = matedec[...]
    neardec = jnp.where(near_is_me, mydec, itsdec)
    fardec = jnp.where(near_is_me, itsdec, mydec)
    for h in range(HEADS):
        mine = st_ref[pl.ds(pl.multiple_of(core * half + h * STATE, STATE), STATE), :]
        its = mate[srows(h), :]
        near = jnp.where(near_is_me, mine.astype(F32), its.astype(F32))
        far = jnp.where(near_is_me, its.astype(F32), mine.astype(F32))
        comb[srows(h), :] = (scaled(fardec, near, h) + far).astype(BF16)
    if not backward:
        both = neardec * fardec
        for j in range(chips):
            first = j * share // STATE
            decout[j, :groups, :] = both[first : first + groups, :]

    def start_in(k, _):
        to = lax.rem(chip + k, chips)
        if not backward:
            dec_copy(to, chip).start()
        in_copy(to, chip).start()
        return 0

    lax.fori_loop(1, chips, start_in, 0)
    inbox[chip] = comb[rows_of(chip, share), :]
    if backward:
        block_copy.start()
        lax.fori_loop(1, n, lambda k, _: (nt_copy(lax.rem(me + k, n), me).start(), 0)[1], 0)
        gotnt_ref[me] = nt_ref[rows_of(me, inner), :]
    else:
        decbox[chip] = decout[chip]
        ring(1)

    def arrive(k, _):
        peer = lax.rem(chip + k, chips)
        if not backward:
            dec_copy(peer, peer).wait_recv()
        in_copy(peer, peer).wait_recv()
        return 0

    lax.fori_loop(1, chips, arrive, 0)

    def scan(k, held):
        i = chips - 1 - k if backward else k
        outbox[i] = held.astype(BF16)

        @pl.when(i != chip)
        def _():
            f_copy(i, chip).start()

        grown = [
            held[g * size : (g + 1) * size] * decbox[i, g : g + 1, :] for g in range(groups)
        ]
        grown = grown[0] if groups == 1 else jnp.concatenate(grown, axis=0)
        return grown + inbox[i].astype(F32)

    lax.fori_loop(0, chips, scan, jnp.zeros((share, LANES), F32))
    fbox[rows_of(chip, share), :] = outbox[chip]

    def landed(k, _):
        peer = lax.rem(chip + k, chips)
        f_copy(peer, peer).wait_recv()
        return 0

    lax.fori_loop(1, chips, landed, 0)
    for h in range(HEADS):
        rows = pl.ds(pl.multiple_of(core * half + h * STATE, STATE), STATE)
        came = fbox[srows(h), :].astype(F32)
        near = jnp.where(near_is_me, st_ref[rows, :].astype(F32), mate[srows(h), :].astype(F32))
        later = scaled(neardec, came, h) + near
        out_ref[rows, :] = jnp.where(near_is_me, came, later).astype(BF16)
        other[srows(h), :] = jnp.where(near_is_me, later, came).astype(BF16)
    last = remote(other, out_ref.at[rows_of(core, half), :], last_send, last_recv, partner)
    last.start()
    if not backward:
        for step in range(2, cw_steps + 1):
            ring(step)

        def mate_block(k, _):
            block = 2 * k + 1 - core
            block_copy_of(0, block, 2, partner).wait_recv()
            block_copy_of(1, block, 2, partner).wait_recv()
            return 0

        lax.fori_loop(0, chips, mate_block, 0)
        for copy in sent:
            copy.wait_send()
        dec_mate.wait_send()

    def finish(k, _):
        peer = lax.rem(chip + k, chips)
        in_copy(peer, chip).wait_send()
        f_copy(peer, chip).wait_send()
        if not backward:
            dec_copy(peer, chip).wait_send()
        return 0

    lax.fori_loop(1, chips, finish, 0)
    if backward:

        def finish_nt(k, _):
            peer = lax.rem(me + k, n)
            nt_copy(peer, peer).wait_recv()
            nt_copy(peer, me).wait_send()
            return 0

        lax.fori_loop(1, n, finish_nt, 0)
    to_mate.wait_send()
    last.wait()
    if backward:
        block_copy.wait()


def exchange(n, backward, *operands):
    chips = n // 2
    share = ROWS // n
    outs = [out_of(ROWS, LANES), out_of(TOK, D) if backward else out_of(n, TOK, D)]
    if backward:
        outs.append(out_of(n, INNER // n, 2 * TOK))
    else:
        outs += [
            out_of(HEADS, LANES, dtype=F32), out_of(chips, 8, LANES, dtype=F32), out_of(n, INNER // n, D)
        ]
    dma = pltpu.SemaphoreType.DMA
    vmem = pl.BlockSpec(memory_space=pltpu.VMEM)
    sems = [dma((2,)), dma((2,)), dma((chips,)), dma((chips,)), dma((chips,)), dma((chips,)), dma, dma, dma, dma]
    if backward:
        sems += [dma((n,)), dma((n,))]
    else:
        sems += [dma((chips,)), dma((chips,))] + [dma((n,))] * 8
    return pl.pallas_call(
        functools.partial(exchange_kernel, n, backward),
        out_shape=outs,
        in_specs=[vmem] * len(operands),
        out_specs=[vmem] * len(outs),
        scratch_shapes=[
            pltpu.VMEM((ROWS // 2, LANES), BF16), pltpu.VMEM((ROWS // 2, LANES), BF16),
            pltpu.VMEM((chips, share, LANES), BF16), pltpu.VMEM((chips, share, LANES), BF16),
            pltpu.VMEM((ROWS // 2, LANES), BF16), pltpu.VMEM((ROWS // 2, LANES), BF16),
            pltpu.VMEM((chips, 8, LANES), F32),
        ] + sems,
        compiler_params=pltpu.CompilerParams(
            collective_id=1 if backward else 0, has_side_effects=True, vmem_limit_bytes=VMEM_LIMIT
        ),
    )(*operands)


def strand_block(*shape):
    return pl.BlockSpec((1,) + shape, lambda s: (s,) + (0,) * len(shape))


def fixed_block(*shape):
    return pl.BlockSpec(shape, lambda s: (0,) * len(shape))


def out_of(*shape, dtype=BF16):
    return jax.ShapeDtypeStruct(shape, dtype)


PARAMS = pltpu.CompilerParams(vmem_limit_bytes=VMEM_LIMIT)


def cost(flops, count):
    return pl.CostEstimate(flops=flops, bytes_accessed=count, transcendentals=0)


def per_device(
    proj_main, proj_state, step_raw, step_bias, decay_log, skip_scale, norm_gain, out_weight, grad_mixed
):
    n = lax.axis_size("seq")
    spare = LANES - HEADS
    raw = jnp.swapaxes(step_raw, 1, 2)
    bias, dlog, skip = (
        jnp.pad(v, (0, spare)).reshape(1, LANES) for v in (step_bias, decay_log, skip_scale)
    )
    gain = norm_gain.reshape(1, INNER)

    main_x = pl.BlockSpec((1, TOK, INNER), lambda s: (s, 0, 0))
    row = fixed_block(1, LANES)
    state_rows = HEADS * STATE
    st, dec = pl.pallas_call(
        local_state_kernel,
        grid=(2,),
        in_specs=[main_x, strand_block(TOK, 2 * STATE), strand_block(HEADS, TOK), row, row],
        out_specs=[strand_block(state_rows, LANES), strand_block(HEADS, LANES)],
        out_shape=[out_of(2, state_rows, LANES), out_of(2, HEADS, LANES, dtype=F32)],
        compiler_params=PARAMS,
    )(proj_main, proj_state, raw, bias, dlog)
    decs = dec.reshape(2 * HEADS, LANES)
    entering, whole_grad, matedec, decbox, whole_weight = exchange(
        n, False, st.reshape(ROWS, LANES), decs, grad_mixed, out_weight
    )
    whole_weight = whole_weight.reshape(INNER, D)
    grad_far = lax.dynamic_index_in_dim(whole_grad, n - 1 - lax.axis_index("seq"), 0, keepdims=False)
    whole_grad = whole_grad.reshape(n * TOK, D)
    entering = entering.reshape(2, state_rows, LANES)

    nt, so, gz, gy, de, gyy = pl.pallas_call(
        middle_kernel,
        grid=(2,),
        in_specs=[
            strand_block(TOK, 2 * INNER), strand_block(TOK, 2 * STATE), strand_block(HEADS, TOK),
            row, row, row, fixed_block(1, INNER), fixed_block(INNER, D), fixed_block(TOK, D),
            fixed_block(TOK, D), strand_block(state_rows, LANES),
        ],
        out_specs=[
            pl.BlockSpec((INNER, TOK), lambda s: (0, s)), strand_block(TOK, D),
            strand_block(TOK, INNER), strand_block(TOK, INNER), strand_block(state_rows, LANES),
            strand_block(TOK, LANES),
        ],
        out_shape=[
            out_of(INNER, 2 * TOK), out_of(2, TOK, D), out_of(2, TOK, INNER), out_of(2, TOK, INNER),
            out_of(2, state_rows, LANES), out_of(2, TOK, LANES, dtype=F32),
        ],
        scratch_shapes=[
            pltpu.VMEM((TOK, INNER), F32), pltpu.VMEM((TOK, INNER), F32),
            pltpu.VMEM((TOK, D), BF16), pltpu.VMEM((TOK, INNER), BF16),
        ],
        compiler_params=PARAMS,
    )(proj_main, proj_state, raw, bias, dlog, skip, gain, whole_weight, grad_mixed, grad_far, entering)

    leaving, so_far, all_nt = exchange(
        n, True, de.reshape(ROWS, LANES), decs, so, matedec, decbox, nt
    )
    leaving = leaving.reshape(2, state_rows, LANES)

    grad_main, grad_state, grad_step = pl.pallas_call(
        last_kernel,
        grid=(2,),
        in_specs=[
            main_x, strand_block(TOK, INNER), strand_block(TOK, INNER), strand_block(TOK, 2 * STATE),
            strand_block(HEADS, TOK), row, row, row, strand_block(state_rows, LANES),
            strand_block(state_rows, LANES), strand_block(TOK, LANES),
        ],
        out_specs=[strand_block(TOK, 2 * INNER), strand_block(TOK, 2 * STATE), strand_block(HEADS, TOK)],
        out_shape=[
            out_of(2, TOK, 2 * INNER), out_of(2, TOK, 2 * STATE, dtype=F32), out_of(2, HEADS, TOK, dtype=F32),
        ],
        scratch_shapes=[pltpu.VMEM((TOK, LANES), F32)],
        compiler_params=PARAMS,
    )(proj_main, gz, gy, proj_state, raw, bias, dlog, skip, entering, leaving, gyy)

    vmem = pl.BlockSpec(memory_space=pltpu.VMEM)
    grad_weight, mixed_out = pl.pallas_call(
        functools.partial(weight_kernel, n),
        in_specs=[vmem] * 4,
        out_specs=[vmem] * 2,
        out_shape=[out_of(INNER // n, D, dtype=F32), out_of(TOK, D)],
        compiler_params=PARAMS,
    )(all_nt, whole_grad, so, so_far)
    return mixed_out, grad_main, grad_state, jnp.swapaxes(grad_step, 1, 2), grad_weight


def solution(mesh):
    placed = (
        P(None, ("parts", "seq"), None), P(None, ("parts", "seq"), None),
        P(None, ("parts", "seq"), None), P(), P(), P(), P(), P("seq", None),
        P(("parts", "seq"), None),
    )
    return jax.shard_map(
        per_device,
        mesh=mesh,
        in_specs=placed,
        out_specs=(
            P(("parts", "seq"), None), P(None, ("parts", "seq"), None),
            P(None, ("parts", "seq"), None), P(None, ("parts", "seq"), None),
            P(("parts", "seq"), None),
        ),
        check_vma=False,
    )
```

```python
import functools

import jax
import jax.numpy as jnp
from jax import lax
from jax.experimental import pallas as pl
from jax.experimental.pallas import tpu as pltpu
from jax.sharding import PartitionSpec as P

D = 1024
HEADS = 16
HEAD_DIM = 128
STATE = 64
INNER = 2048
TOK = 128
LANES = 128
ROWS = 2 * HEADS * STATE
EPSILON = 1e-05
HIGH = lax.Precision.HIGHEST
F32 = jnp.float32
BF16 = jnp.bfloat16
MESH = pl.DeviceIdType.MESH
VMEM_LIMIT = 56 * 2**20


def dot(a, b, ca=1, cb=0, precision=None):
    return lax.dot_general(
        a, b, (((ca,), (cb,)), ((), ())), precision=precision, preferred_element_type=F32
    )


def grids(shape=(TOK, TOK)):
    return lax.broadcasted_iota(jnp.int32, shape, 0), lax.broadcasted_iota(jnp.int32, shape, 1)


def anti_identity():
    row, col = grids()
    return (row + col == TOK - 1).astype(BF16)


def flip_both(block):
    anti = anti_identity()
    turned = dot(anti, block).astype(BF16)
    count = block.shape[1] // TOK
    parts = [
        dot(turned[:, (count - 1 - k) * TOK : (count - k) * TOK], anti).astype(BF16)
        for k in range(count)
    ]
    return jnp.concatenate(parts, axis=1)


def steps(raw_t, bias, dlog):
    raw = jnp.concatenate([raw_t, jnp.zeros((LANES - HEADS, TOK), F32)], axis=0).T
    arg = raw + bias
    size = jnp.maximum(arg, 0.0) + jnp.log1p(jnp.exp(-jnp.abs(arg)))
    rate = -jnp.exp(dlog) * size
    row, col = grids()
    lower = (row >= col).astype(F32)
    cum = dot(lower, rate, precision=HIGH)
    return arg, size, rate, cum


def head(h):
    return slice(h * HEAD_DIM, (h + 1) * HEAD_DIM)


def srows(h):
    return slice(h * STATE, (h + 1) * STATE)


def local_state_kernel(x_ref, bc_ref, raw_ref, bias_ref, dlog_ref, st_ref, dec_ref):
    _, size, _, cum = steps(raw_ref[0], bias_ref[...], dlog_ref[...])
    total = cum[TOK - 1 : TOK, :]
    weight = jnp.exp(total - cum) * size
    b = bc_ref[0, :, :STATE]
    for h in range(HEADS):
        xw = (x_ref[0, :, head(h)].astype(F32) * weight[:, h : h + 1]).astype(BF16)
        st_ref[0, srows(h), :] = dot(b, xw, 0, 0).astype(BF16)
    dec_ref[0] = jnp.broadcast_to(jnp.exp(cum.T[:HEADS, TOK - 1 :]), (HEADS, LANES))


def mixing(scores, mask, cum, cum_t, size_t, h):
    gap = cum[:, h : h + 1] - cum_t[h : h + 1, :]
    decay = jnp.where(mask, jnp.exp(jnp.minimum(gap, 0.0)), 0.0)
    return decay * size_t[h : h + 1, :]


def middle_kernel(
    main_ref, bc_ref, raw_ref, bias_ref, dlog_ref, skip_ref, gain_ref, w_ref, gm_ref, gmm_ref, e_ref,
    nt_ref, so_ref, gz_ref, gy_ref, de_ref, gyy_ref,
    y_s, gn_s, bi_s, no_s,
):
    strand = pl.program_id(0)

    @pl.when(strand == 0)
    def _():
        bi_s[...] = gm_ref[...]

    @pl.when(strand == 1)
    def _():
        bi_s[...] = flip_both(gmm_ref[...])

    gn_s[...] = dot(bi_s[...], w_ref[...], 1, 1) * gain_ref[...]
    _, size, _, cum = steps(raw_ref[0], bias_ref[...], dlog_ref[...])
    cum_t, size_t = cum.T, size.T
    ecum = jnp.exp(cum)
    b, c = bc_ref[0, :, :STATE], bc_ref[0, :, STATE:]
    scores = dot(c, b, 1, 1)
    row, col = grids()
    mask = row >= col
    squares = jnp.zeros((TOK, LANES), F32)
    crossed = jnp.zeros((TOK, LANES), F32)
    for h in range(HEADS):
        m = (scores * mixing(scores, mask, cum, cum_t, size_t, h)).astype(BF16)
        x = main_ref[0, :, head(h)]
        y = dot(m, x) + ecum[:, h : h + 1] * dot(c, e_ref[0, srows(h), :])
        y = y + skip_ref[0:1, h : h + 1] * x.astype(F32)
        y_s[:, head(h)] = y
        z = main_ref[0, :, INNER + h * HEAD_DIM : INNER + (h + 1) * HEAD_DIM].astype(F32)
        gated = y * (z / (1.0 + jnp.exp(-z)))
        squares += gated * gated
        crossed += gated * gn_s[:, head(h)]
    r = lax.rsqrt(jnp.sum(squares, axis=1, keepdims=True) / INNER + EPSILON)
    factor = r * r * r * (jnp.sum(crossed, axis=1, keepdims=True) / INNER)
    spin = jnp.where(strand == 0, (row == col).astype(F32), (row + col == TOK - 1).astype(F32))
    spin = spin.astype(BF16)
    for h in range(HEADS):
        z = main_ref[0, :, INNER + h * HEAD_DIM : INNER + (h + 1) * HEAD_DIM].astype(F32)
        y = y_s[:, head(h)]
        sig = 1.0 / (1.0 + jnp.exp(-z))
        silu = z * sig
        gated = y * silu
        normed = (gated * r * gain_ref[:, head(h)]).astype(BF16)
        no_s[:, head(h)] = normed
        nt_ref[head(h), :] = dot(normed, spin, 0, 0).astype(BF16)
        dgated = r * gn_s[:, head(h)] - gated * factor
        gz_ref[0, :, head(h)] = (dgated * y * (sig * (1.0 + z * (1.0 - sig)))).astype(BF16)
        gy = (dgated * silu).astype(BF16)
        gy_ref[0, :, head(h)] = gy
        gyf = gy.astype(F32)
        scan_y = y - skip_ref[0:1, h : h + 1] * main_ref[0, :, head(h)].astype(F32)
        gyy_ref[0, :, h : h + 1] = jnp.sum(gyf * scan_y, axis=1, keepdims=True)
        de_ref[0, srows(h), :] = dot(c, (gyf * ecum[:, h : h + 1]).astype(BF16), 0, 0).astype(BF16)
    so_ref[0] = dot(no_s[...], w_ref[...]).astype(BF16)


def last_kernel(
    x_ref, gz_ref, gy_ref, bc_ref, raw_ref, bias_ref, dlog_ref, skip_ref, e_ref, lv_ref, gyy_ref,
    gmain_ref, gstate_ref, gstep_ref,
    xdx_s,
):
    arg, size, _, cum = steps(raw_ref[0], bias_ref[...], dlog_ref[...])
    cum_t, size_t = cum.T, size.T
    ecum = jnp.exp(cum)
    total = cum[TOK - 1 : TOK, :]
    weight = jnp.exp(total - cum) * size
    b, c = bc_ref[0, :, :STATE], bc_ref[0, :, STATE:]
    scores = dot(c, b, 1, 1)
    row, col = grids()
    mask = row >= col
    lane = lax.broadcasted_iota(jnp.int32, (1, LANES), 1)
    gscore = jnp.zeros((TOK, TOK), F32)
    gb = jnp.zeros((TOK, STATE), F32)
    gc = jnp.zeros((TOK, STATE), F32)
    gtotal = jnp.zeros((1, LANES), F32)
    xdx_s[...] = jnp.zeros_like(xdx_s)
    for h in range(HEADS):
        w = mixing(scores, mask, cum, cum_t, size_t, h)
        m = (scores * w).astype(BF16)
        x, gy = x_ref[0, :, head(h)], gy_ref[0, :, head(h)]
        xf, gyf = x.astype(F32), gy.astype(F32)
        lv, e = lv_ref[srows(h), :], e_ref[srows(h), :]
        gscore += dot(gy, x, 1, 1) * w
        wcol = weight[:, h : h + 1]
        through = wcol * dot(b, lv)
        dx = dot(m, gy, 0, 0) + through
        gmain_ref[0, :, head(h)] = (dx + skip_ref[0:1, h : h + 1] * gyf).astype(BF16)
        xdx_s[:, h : h + 1] = jnp.sum(xf * dx, axis=1, keepdims=True)
        gc += dot((gyf * ecum[:, h : h + 1]).astype(BF16), e, 1, 1)
        gb += dot((xf * wcol).astype(BF16), lv, 1, 1)
        held = jnp.sum(xf * through, axis=0, keepdims=True)
        kept = jnp.sum(e.astype(F32) * lv.astype(F32), axis=0, keepdims=True)
        both = jnp.sum(held + jnp.exp(total[:, h : h + 1]) * kept, axis=1, keepdims=True)
        gtotal += jnp.where(lane == h, both, 0.0)
    gs = gscore.astype(BF16)
    gstate_ref[0, :, :STATE] = gb + dot(gs, c, 0, 0)
    gstate_ref[0, :, STATE:] = gc + dot(gs, b)
    gmain_ref[0, :, INNER:] = gz_ref[0]
    real = lane < HEADS
    gcum = jnp.where(real, gyy_ref[0], 0.0) - xdx_s[...]
    upper = (row <= col).astype(F32)
    grate = dot(upper, gcum, precision=HIGH) + gtotal
    gsize = xdx_s[...] / size - jnp.exp(dlog_ref[...]) * grate
    gstep_ref[0] = (gsize / (1.0 + jnp.exp(-arg))).T[:HEADS]


def weight_kernel(n, nt_ref, gm_ref, so_ref, som_ref, gw_ref, mixed_ref):
    near = jnp.concatenate([nt_ref[i, :, :TOK] for i in range(n)], axis=1)
    far = jnp.concatenate([nt_ref[n - 1 - i, :, TOK:] for i in range(n)], axis=1)
    plain = dot(near, gm_ref[...])
    turned = dot(far, gm_ref[...])
    row, col = grids()
    anti = (row + col == TOK - 1).astype(F32)
    count = D // TOK
    for k in range(count):
        back = turned[:, (count - 1 - k) * TOK : (count - k) * TOK]
        gw_ref[:, k * TOK : (k + 1) * TOK] = plain[:, k * TOK : (k + 1) * TOK] + dot(
            back, anti, precision=HIGH
        )
    mixed_ref[...] = (so_ref[0].astype(F32) + flip_both(som_ref[...]).astype(F32)).astype(BF16)


def exchange_kernel(n, backward, *refs):
    if backward:
        (st_ref, dec_ref, block_ref, matedec, decbox, nt_ref) = refs[:6]
        step_ins = refs[6:16]
        gotblock_ref, gotnt_ref = refs[16:18]
        step_outs = refs[18:21]
        out_ref, xdx_s = refs[21:23]
        rest = refs[23:]
    else:
        (st_ref, dec_ref, g_ref, w_ref, out_ref, gall_ref, matedec, decbox, wall_ref) = refs[:9]
        rest = refs[9:]
    (mate, comb, inbox, outbox, fbox, other, decout), sems = rest[:7], rest[7:]
    (mate_send, mate_recv, in_send, in_recv, f_send, f_recv, last_send, last_recv, block_send, block_recv) = sems[:10]
    extra = sems[10:]
    me = lax.axis_index("seq")
    chips = n // 2
    chip, core = me // 2, lax.rem(me, 2)
    partner = me + 1 - 2 * core
    half = ROWS // 2
    share = half // chips
    inner = INNER // n
    groups = max(1, share // STATE)
    size = share // groups
    barrier = pltpu.get_barrier_semaphore()

    def greet(k, _):
        pl.semaphore_signal(
            barrier, inc=1, device_id={"seq": lax.rem(me + k, n)}, device_id_type=MESH
        )
        return 0

    lax.fori_loop(1, n, greet, 0)
    pl.semaphore_wait(barrier, n - 1)

    def rows_of(i, count):
        return pl.ds(pl.multiple_of(i * count, count), count)

    def remote(src, dst, send, recv, to):
        return pltpu.make_async_remote_copy(
            src_ref=src, dst_ref=dst, send_sem=send, recv_sem=recv,
            device_id={"seq": to}, device_id_type=MESH,
        )

    to_mate = remote(st_ref.at[rows_of(1 - core, half), :], mate, mate_send.at[0], mate_recv.at[0], partner)
    to_mate.start()
    dec_mate = None
    if not backward:
        dec_mate = remote(dec_ref.at[rows_of(1 - core, HEADS), :], matedec, mate_send.at[1], mate_recv.at[1], partner)
        dec_mate.start()

    def in_copy(to, slot):
        return remote(
            comb.at[rows_of(to, share), :], inbox.at[slot], in_send.at[to], in_recv.at[slot], 2 * to + core
        )

    def dec_copy(to, slot):
        return remote(decout.at[to], decbox.at[slot], extra[0].at[to], extra[1].at[slot], 2 * to + core)

    def f_copy(to, slot):
        return remote(
            outbox.at[to], fbox.at[rows_of(slot, share), :], f_send.at[to], f_recv.at[slot], 2 * to + core
        )

    def nt_copy(to, slot):
        return remote(
            nt_ref.at[rows_of(to, inner), :], gotnt_ref.at[slot], extra[0].at[to], extra[1].at[slot], to
        )

    if backward:
        block_copy = remote(block_ref.at[1], gotblock_ref, block_send, block_recv, n - 1 - me)

    if not backward:
        place = jnp.where(lax.rem(chip, 2) == 0, chip // 2, chips - 1 - chip // 2)

        def at(offset):
            pos = lax.rem(place + offset + 2 * chips, chips)
            return jnp.where(pos < chips // 2, 2 * pos, 2 * (chips - 1 - pos) + 1)

        right, left = 2 * at(1) + core, 2 * at(-1) + core
        cw_steps = chips // 2
        ccw_steps = chips - 1 - cw_steps
        sent = []

        def launch(copy):
            copy.start()
            sent.append(copy)

        def block_copy_of(which, block, lane, to):
            whole, sems_ = ((wall_ref, extra[2:6]), (gall_ref, extra[6:10]))[which]
            return remote(whole.at[block], whole.at[block], sems_[lane].at[block], sems_[3].at[block], to)

        def ring_of(which, step):
            for lane, count, sign, to in ((0, cw_steps, -1, right), (1, ccw_steps, 1, left)):
                if step > count:
                    continue
                block = 2 * at(sign * step) + core
                if step > 0:
                    block_copy_of(which, block, lane, to).wait_recv()
                if step < count:
                    launch(block_copy_of(which, block, lane, to))
                if step > 0 or lane == 0:
                    launch(block_copy_of(which, block, 2, partner))

        def ring(step):
            ring_of(0, step)
            ring_of(1, step)

        wall_ref[me] = w_ref[...]
        gall_ref[me] = g_ref[...]
        ring(0)

    def scaled(dec, rows, h):
        return dec[h : h + 1, :] * rows.astype(F32)

    near_is_me = core == (1 if backward else 0)
    to_mate.wait_recv()
    if not backward:
        dec_mate.wait_recv()
    mydec = dec_ref[rows_of(core, HEADS), :]
    itsdec = matedec[...]
    neardec = jnp.where(near_is_me, mydec, itsdec)
    fardec = jnp.where(near_is_me, itsdec, mydec)
    for h in range(HEADS):
        mine = st_ref[pl.ds(pl.multiple_of(core * half + h * STATE, STATE), STATE), :]
        its = mate[srows(h), :]
        near = jnp.where(near_is_me, mine.astype(F32), its.astype(F32))
        far = jnp.where(near_is_me, its.astype(F32), mine.astype(F32))
        comb[srows(h), :] = (scaled(fardec, near, h) + far).astype(BF16)
    if not backward:
        both = neardec * fardec
        for j in range(chips):
            first = j * share // STATE
            decout[j, :groups, :] = both[first : first + groups, :]

    def start_in(k, _):
        to = lax.rem(chip + k, chips)
        if not backward:
            dec_copy(to, chip).start()
        in_copy(to, chip).start()
        return 0

    lax.fori_loop(1, chips, start_in, 0)
    inbox[chip] = comb[rows_of(chip, share), :]
    if backward:
        block_copy.start()
        lax.fori_loop(1, n, lambda k, _: (nt_copy(lax.rem(me + k, n), me).start(), 0)[1], 0)
        gotnt_ref[me] = nt_ref[rows_of(me, inner), :]
    else:
        decbox[chip] = decout[chip]
        ring(1)

    def arrive(k, _):
        peer = lax.rem(chip + k, chips)
        if not backward:
            dec_copy(peer, peer).wait_recv()
        in_copy(peer, peer).wait_recv()
        return 0

    lax.fori_loop(1, chips, arrive, 0)

    def scan(k, held):
        i = chips - 1 - k if backward else k
        outbox[i] = held.astype(BF16)

        @pl.when(i != chip)
        def _():
            f_copy(i, chip).start()

        grown = [
            held[g * size : (g + 1) * size] * decbox[i, g : g + 1, :] for g in range(groups)
        ]
        grown = grown[0] if groups == 1 else jnp.concatenate(grown, axis=0)
        return grown + inbox[i].astype(F32)

    lax.fori_loop(0, chips, scan, jnp.zeros((share, LANES), F32))
    fbox[rows_of(chip, share), :] = outbox[chip]

    def landed(k, _):
        peer = lax.rem(chip + k, chips)
        f_copy(peer, peer).wait_recv()
        return 0

    lax.fori_loop(1, chips, landed, 0)
    for h in range(HEADS):
        rows = pl.ds(pl.multiple_of(core * half + h * STATE, STATE), STATE)
        came = fbox[srows(h), :].astype(F32)
        near = jnp.where(near_is_me, st_ref[rows, :].astype(F32), mate[srows(h), :].astype(F32))
        later = scaled(neardec, came, h) + near
        out_ref[rows, :] = jnp.where(near_is_me, came, later).astype(BF16)
        other[srows(h), :] = jnp.where(near_is_me, later, came).astype(BF16)
    last = remote(other, out_ref.at[rows_of(core, half), :], last_send, last_recv, partner)
    last.start()
    if not backward:
        for step in range(2, cw_steps + 1):
            ring(step)

        def mate_block(k, _):
            block = 2 * k + 1 - core
            block_copy_of(0, block, 2, partner).wait_recv()
            block_copy_of(1, block, 2, partner).wait_recv()
            return 0

        lax.fori_loop(0, chips, mate_block, 0)
        for copy in sent:
            copy.wait_send()
        dec_mate.wait_send()

    def finish(k, _):
        peer = lax.rem(chip + k, chips)
        in_copy(peer, chip).wait_send()
        f_copy(peer, chip).wait_send()
        if not backward:
            dec_copy(peer, chip).wait_send()
        return 0

    lax.fori_loop(1, chips, finish, 0)
    if backward:
        last.wait()
        main_ref, gz_ref, gy_ref, bc_ref, raw_ref, bias_ref, dlog_ref, skip_ref, e_ref, gyy_ref = step_ins

        def strand(s, _):
            one = pl.ds(s, 1)
            rows = rows_of(s, half)
            last_kernel(
                main_ref.at[one], gz_ref.at[one], gy_ref.at[one], bc_ref.at[one], raw_ref.at[one],
                bias_ref, dlog_ref, skip_ref, e_ref.at[rows, :], out_ref.at[rows, :], gyy_ref.at[one],
                *[ref.at[one] for ref in step_outs], xdx_s,
            )
            return 0

        lax.fori_loop(0, 2, strand, 0)

        def finish_nt(k, _):
            peer = lax.rem(me + k, n)
            nt_copy(peer, peer).wait_recv()
            nt_copy(peer, me).wait_send()
            return 0

        lax.fori_loop(1, n, finish_nt, 0)
    to_mate.wait_send()
    if backward:
        block_copy.wait()
    else:
        last.wait()


def exchange(n, backward, *operands):
    chips = n // 2
    share = ROWS // n
    scratch = []
    if backward:
        outs = [
            out_of(TOK, D), out_of(n, INNER // n, 2 * TOK), out_of(2, TOK, 2 * INNER),
            out_of(2, TOK, 2 * STATE, dtype=F32), out_of(2, HEADS, TOK, dtype=F32),
        ]
        scratch = [pltpu.VMEM((ROWS, LANES), BF16), pltpu.VMEM((TOK, LANES), F32)]
    else:
        outs = [
            out_of(ROWS, LANES), out_of(n, TOK, D),
            out_of(HEADS, LANES, dtype=F32), out_of(chips, 8, LANES, dtype=F32), out_of(n, INNER // n, D)
        ]
    dma = pltpu.SemaphoreType.DMA
    vmem = pl.BlockSpec(memory_space=pltpu.VMEM)
    sems = [dma((2,)), dma((2,)), dma((chips,)), dma((chips,)), dma((chips,)), dma((chips,)), dma, dma, dma, dma]
    if backward:
        sems += [dma((n,)), dma((n,))]
    else:
        sems += [dma((chips,)), dma((chips,))] + [dma((n,))] * 8
    return pl.pallas_call(
        functools.partial(exchange_kernel, n, backward),
        out_shape=outs,
        in_specs=[vmem] * len(operands),
        out_specs=[vmem] * len(outs),
        scratch_shapes=scratch + [
            pltpu.VMEM((ROWS // 2, LANES), BF16), pltpu.VMEM((ROWS // 2, LANES), BF16),
            pltpu.VMEM((chips, share, LANES), BF16), pltpu.VMEM((chips, share, LANES), BF16),
            pltpu.VMEM((ROWS // 2, LANES), BF16), pltpu.VMEM((ROWS // 2, LANES), BF16),
            pltpu.VMEM((chips, 8, LANES), F32),
        ] + sems,
        compiler_params=pltpu.CompilerParams(
            collective_id=1 if backward else 0, has_side_effects=True, vmem_limit_bytes=VMEM_LIMIT
        ),
    )(*operands)


def strand_block(*shape):
    return pl.BlockSpec((1,) + shape, lambda s: (s,) + (0,) * len(shape))


def fixed_block(*shape):
    return pl.BlockSpec(shape, lambda s: (0,) * len(shape))


def out_of(*shape, dtype=BF16):
    return jax.ShapeDtypeStruct(shape, dtype)


PARAMS = pltpu.CompilerParams(vmem_limit_bytes=VMEM_LIMIT)


def cost(flops, count):
    return pl.CostEstimate(flops=flops, bytes_accessed=count, transcendentals=0)


def per_device(
    proj_main, proj_state, step_raw, step_bias, decay_log, skip_scale, norm_gain, out_weight, grad_mixed
):
    n = lax.axis_size("seq")
    spare = LANES - HEADS
    raw = jnp.swapaxes(step_raw, 1, 2)
    bias, dlog, skip = (
        jnp.pad(v, (0, spare)).reshape(1, LANES) for v in (step_bias, decay_log, skip_scale)
    )
    gain = norm_gain.reshape(1, INNER)

    main_x = pl.BlockSpec((1, TOK, INNER), lambda s: (s, 0, 0))
    row = fixed_block(1, LANES)
    state_rows = HEADS * STATE
    st, dec = pl.pallas_call(
        local_state_kernel,
        grid=(2,),
        in_specs=[main_x, strand_block(TOK, 2 * STATE), strand_block(HEADS, TOK), row, row],
        out_specs=[strand_block(state_rows, LANES), strand_block(HEADS, LANES)],
        out_shape=[out_of(2, state_rows, LANES), out_of(2, HEADS, LANES, dtype=F32)],
        compiler_params=PARAMS,
    )(proj_main, proj_state, raw, bias, dlog)
    decs = dec.reshape(2 * HEADS, LANES)
    entering, whole_grad, matedec, decbox, whole_weight = exchange(
        n, False, st.reshape(ROWS, LANES), decs, grad_mixed, out_weight
    )
    whole_weight = whole_weight.reshape(INNER, D)
    grad_far = lax.dynamic_index_in_dim(whole_grad, n - 1 - lax.axis_index("seq"), 0, keepdims=False)
    whole_grad = whole_grad.reshape(n * TOK, D)
    entering = entering.reshape(2, state_rows, LANES)

    nt, so, gz, gy, de, gyy = pl.pallas_call(
        middle_kernel,
        grid=(2,),
        in_specs=[
            strand_block(TOK, 2 * INNER), strand_block(TOK, 2 * STATE), strand_block(HEADS, TOK),
            row, row, row, fixed_block(1, INNER), fixed_block(INNER, D), fixed_block(TOK, D),
            fixed_block(TOK, D), strand_block(state_rows, LANES),
        ],
        out_specs=[
            pl.BlockSpec((INNER, TOK), lambda s: (0, s)), strand_block(TOK, D),
            strand_block(TOK, INNER), strand_block(TOK, INNER), strand_block(state_rows, LANES),
            strand_block(TOK, LANES),
        ],
        out_shape=[
            out_of(INNER, 2 * TOK), out_of(2, TOK, D), out_of(2, TOK, INNER), out_of(2, TOK, INNER),
            out_of(2, state_rows, LANES), out_of(2, TOK, LANES, dtype=F32),
        ],
        scratch_shapes=[
            pltpu.VMEM((TOK, INNER), F32), pltpu.VMEM((TOK, INNER), F32),
            pltpu.VMEM((TOK, D), BF16), pltpu.VMEM((TOK, INNER), BF16),
        ],
        compiler_params=PARAMS,
    )(proj_main, proj_state, raw, bias, dlog, skip, gain, whole_weight, grad_mixed, grad_far, entering)

    so_far, all_nt, grad_main, grad_state, grad_step = exchange(
        n, True, de.reshape(ROWS, LANES), decs, so, matedec, decbox, nt,
        proj_main, gz, gy, proj_state, raw, bias, dlog, skip, entering.reshape(ROWS, LANES), gyy,
    )

    vmem = pl.BlockSpec(memory_space=pltpu.VMEM)
    grad_weight, mixed_out = pl.pallas_call(
        functools.partial(weight_kernel, n),
        in_specs=[vmem] * 4,
        out_specs=[vmem] * 2,
        out_shape=[out_of(INNER // n, D, dtype=F32), out_of(TOK, D)],
        compiler_params=PARAMS,
    )(all_nt, whole_grad, so, so_far)
    return mixed_out, grad_main, grad_state, jnp.swapaxes(grad_step, 1, 2), grad_weight


def solution(mesh):
    placed = (
        P(None, ("parts", "seq"), None), P(None, ("parts", "seq"), None),
        P(None, ("parts", "seq"), None), P(), P(), P(), P(), P("seq", None),
        P(("parts", "seq"), None),
    )
    return jax.shard_map(
        per_device,
        mesh=mesh,
        in_specs=placed,
        out_specs=(
            P(("parts", "seq"), None), P(None, ("parts", "seq"), None),
            P(None, ("parts", "seq"), None), P(None, ("parts", "seq"), None),
            P(("parts", "seq"), None),
        ),
        check_vma=False,
    )
```
